256 devices in a mesh: dp: 8 (over y, z_lo), tensor: 32 (over z_hi, x, core).
Axes of the slice: x: 4, y: 4, z: 8 (z_hi: 4, z_lo: 2; z = z_hi * 2 + z_lo), core: 2. Of those that a mesh axis runs over, the one named last changes fastest.
Arguments:
- gradient_parts: bfloat16 [8, 16384, 4096], P('dp', 'tensor'), may hold values from -1.5 to 1.5
- block_owner: int32 [64], replicated, may hold values from 0 to 63, as said below
- refresh_list: int32 [32], replicated, may hold values from 0 to 63, as said below
- first_moment: bfloat16 [64, 2, 512, 1024], P('tensor', None, 'dp'), may hold values from -4 to 4
- second_moment: bfloat16 [64, 2, 512, 1024], P('tensor', None, 'dp'), may hold values from 0.0039978027 to 0.099609375
- left_statistic: float32 [64, 2, 512, 1024], P('tensor', None, 'dp'), may hold values from -1 to 16
- right_statistic: float32 [64, 2, 512, 1024], P('tensor', None, 'dp'), may hold values from -1 to 16
- left_basis: bfloat16 [64, 2, 512, 1024], P('tensor', None, 'dp'), may hold values from -0.5 to 1.5
- right_basis: bfloat16 [64, 2, 512, 1024], P('tensor', None, 'dp'), may hold values from -0.5 to 1.5
Outputs:
- update: bfloat16 [64, 2, 512, 1024], P('tensor', None, 'dp')
- first_moment_next: bfloat16 [64, 2, 512, 1024], P('tensor', None, 'dp')
- second_moment_next: bfloat16 [64, 2, 512, 1024], P('tensor', None, 'dp')
- left_statistic_next: float32 [64, 2, 512, 1024], P('tensor', None, 'dp')
- right_statistic_next: float32 [64, 2, 512, 1024], P('tensor', None, 'dp')
- left_basis_next: bfloat16 [64, 2, 512, 1024], P('tensor', None, 'dp')
- right_basis_next: bfloat16 [64, 2, 512, 1024], P('tensor', None, 'dp')
The draws below stay inside these ranges and needn't reach their ends.
Inputs may be any that keep to these rules, and one draw needn't show every extreme that they name: A permutation: block b sits at position block_owner[b], on index block_owner[b] // 2 of tensor. `refresh_list`: 32 different block ids; in every draw some index of tensor holds two of them.
All inputs are finite; a program needn't handle non-finite values.
Results may differ from the reference program's by a relative error of at most 0.02.
Values may be sent and summed in bfloat16 or wider, within the bound.
No kernel may reach another device: no remote copies, remote signals or barrier semaphores. Data moves between devices by JAX's collectives and lax.ppermute only.
A program may use at most 192 MiB of HBM per device.

```python
import math
import jax
import jax.numpy as jnp
from jax import lax

BLOCK = 1024
HIDDEN_WIN = 16384
WIDTH_WIN = 4096
NB = 64
SLOTS = 2
N_DP = 8
N_TENSOR = 32


def shared_layout(key):
    ordering = jax.random.permutation(key, NB).astype(jnp.int32)
    busiest = jax.random.randint(jax.random.fold_in(key, 5), (), 0, N_TENSOR).astype(jnp.int32)
    others = jax.random.permutation(jax.random.fold_in(key, 6), NB - SLOTS)[:N_TENSOR - 2].astype(jnp.int32)
    others = jnp.where(others >= busiest * SLOTS, others + SLOTS, others)
    chosen = jnp.concatenate([busiest * SLOTS + jnp.arange(2, dtype=jnp.int32), others])
    position_block = jnp.argsort(ordering).astype(jnp.int32)
    return (ordering, position_block[chosen])


def draw_block_owner(key, part):
    return shared_layout(key)[0]


def draw_refresh_list(key, part):
    return shared_layout(key)[1]


def statistic_blocks(key, lowest, highest, coupling):
    scales = jnp.exp(jax.random.uniform(jax.random.fold_in(key, 11), (NB, BLOCK), jnp.float32, math.log(lowest), math.log(highest)))
    mixture = jax.random.uniform(jax.random.fold_in(key, 12), (NB, BLOCK, BLOCK), jnp.float32, -1.0, 1.0)
    mirror = 0.5 * (mixture + jnp.swapaxes(mixture, 1, 2))
    identity = jnp.eye(BLOCK, dtype=jnp.float32)
    coupled = identity + coupling / BLOCK * mirror * (1.0 - identity)
    root_scale = jnp.sqrt(scales)
    blocks = root_scale[:, :, None] * coupled * root_scale[:, None, :]
    return blocks.reshape(NB, 2, BLOCK // 2, BLOCK)


def basis_blocks(key, strength):
    normal_part = jax.random.normal(jax.random.fold_in(key, 31), (NB, BLOCK, BLOCK), jnp.float32)
    mixture = normal_part
    skewed = strength / math.sqrt(BLOCK) * (mixture - jnp.swapaxes(mixture, 1, 2))
    frames = jnp.eye(BLOCK, dtype=jnp.float32) + skewed
    return frames.reshape(NB, 2, BLOCK // 2, BLOCK).astype(jnp.bfloat16)


def draw_left_statistic(key, part):
    key = jax.random.fold_in(key, 21)
    return statistic_blocks(key, 1.0, 10.0, 0.7)


def draw_right_statistic(key, part):
    key = jax.random.fold_in(key, 22)
    return statistic_blocks(key, 1.0, 10.0, 0.7)


def draw_left_basis(key, part):
    key = jax.random.fold_in(key, 23)
    return basis_blocks(key, 0.15)


def draw_right_basis(key, part):
    key = jax.random.fold_in(key, 24)
    return basis_blocks(key, 0.15)


def level_of(stream_key, shape, pieces, low, high):
    level, own = 1.0, jax.random.fold_in(stream_key, 6)
    for position, shards_of in pieces:
        heights = jnp.exp(jax.random.uniform(jax.random.fold_in(own, position), (shards_of,), jnp.float32, low / len(pieces), high / len(pieces)))
        level = level * jnp.repeat(heights, shape[position] // shards_of).reshape([-1 if axis == position else 1 for axis in range(len(shape))])
    return level


def bell_draw(key, extent, spread, bound, pieces=(), kind=jnp.bfloat16):
    loudness = level_of(key, extent, pieces, -0.22, 0.18) if pieces else 1.0
    drawn = jax.random.normal(key, extent, jnp.float32) * spread * loudness
    return jnp.minimum(jnp.maximum(drawn, -bound), bound).astype(kind)


def setup_inputs(seed: int = 0) -> dict:
    splits = jax.random.split(jax.random.key(seed), 10)
    return {
        "gradient_parts": bell_draw(splits[0], (N_DP, HIDDEN_WIN, WIDTH_WIN), 0.1, 1.5, ((0, 8), (1, 32))),
        "block_owner": draw_block_owner(jax.random.fold_in(splits[9], 71), 0),
        "refresh_list": draw_refresh_list(jax.random.fold_in(splits[9], 71), 0),
        "first_moment": bell_draw(splits[3], (NB, 2, BLOCK // 2, BLOCK), 0.3, 4.0, ((0, 32), (2, 8))),
        "second_moment": jnp.clip(jnp.exp(math.log(0.099609375) - 3.2155114 * jax.random.uniform(splits[4], (NB, 2, BLOCK // 2, BLOCK), jnp.float32) ** level_of(splits[4], (NB, 2, BLOCK // 2, BLOCK), ((0, 32), (2, 8)), -0.2, 0.2)), 0.0039978027, 0.099609375).astype(jnp.bfloat16),
        "left_statistic": draw_left_statistic(jax.random.fold_in(splits[9], 71), 0),
        "right_statistic": draw_right_statistic(jax.random.fold_in(splits[9], 71), 0),
        "left_basis": draw_left_basis(jax.random.fold_in(splits[9], 71), 0),
        "right_basis": draw_right_basis(jax.random.fold_in(splits[9], 71), 0),
    }


BETA_MOMENT = 0.9
BETA_SQUARE = 0.95
BETA_STATS = 0.95
EPSILON = 1e-08

def renew_frame(inputs):
    statistic, old_frame = inputs
    power_step = jnp.dot(statistic.astype(jnp.float32), old_frame.astype(jnp.float32), precision=lax.Precision.HIGHEST, preferred_element_type=jnp.float32).astype(jnp.bfloat16)
    gram_matrix = jnp.dot(power_step.T.astype(jnp.float32), power_step.astype(jnp.float32), preferred_element_type=jnp.float32)
    factor = jnp.linalg.cholesky(gram_matrix)
    solved = lax.linalg.triangular_solve(factor, power_step.astype(jnp.float32).T, left_side=True, lower=True)
    return solved.T.astype(jnp.bfloat16)

def reference(gradient_parts, block_owner, refresh_list, first_moment, second_moment, left_statistic, right_statistic, left_basis, right_basis):
    grad_sum = lax.optimization_barrier(jnp.sum(gradient_parts.astype(jnp.float32), axis=0)).astype(jnp.bfloat16)
    block_total = first_moment.shape[0]
    block_size = first_moment.shape[3]
    block_cols = grad_sum.shape[1] // block_size
    position_block = jnp.argsort(block_owner).astype(jnp.int32)

    def square(values):
        return values.reshape(block_total, block_size, block_size)

    def advance(inputs):
        block_id, moment, second, left_stat_block, right_stat_block, left_frame, right_frame = inputs
        row_start = (block_id // block_cols * block_size).astype(jnp.int32)
        column_start = (block_id % block_cols * block_size).astype(jnp.int32)
        gradient = lax.dynamic_slice(grad_sum, (row_start, column_start), (block_size, block_size))
        turned = jnp.dot(left_frame.T.astype(jnp.float32), gradient.astype(jnp.float32), preferred_element_type=jnp.float32).astype(jnp.bfloat16)
        rotated = jnp.dot(turned.astype(jnp.float32), right_frame.astype(jnp.float32), preferred_element_type=jnp.float32)
        moment = BETA_MOMENT * moment.astype(jnp.float32) + (1.0 - BETA_MOMENT) * rotated
        second = BETA_SQUARE * second.astype(jnp.float32) + (1.0 - BETA_SQUARE) * rotated * rotated
        direction = (moment / (jnp.sqrt(second) + EPSILON)).astype(jnp.bfloat16)
        returned = jnp.dot(direction.astype(jnp.float32), right_frame.T.astype(jnp.float32), preferred_element_type=jnp.float32).astype(jnp.bfloat16)
        update = jnp.dot(left_frame.astype(jnp.float32), returned.astype(jnp.float32), preferred_element_type=jnp.float32).astype(jnp.bfloat16)
        left_stat_block = BETA_STATS * left_stat_block + (1.0 - BETA_STATS) * jnp.dot(gradient.astype(jnp.float32), gradient.T.astype(jnp.float32), preferred_element_type=jnp.float32)
        right_stat_block = BETA_STATS * right_stat_block + (1.0 - BETA_STATS) * jnp.dot(gradient.T.astype(jnp.float32), gradient.astype(jnp.float32), preferred_element_type=jnp.float32)
        return (update, moment.astype(jnp.bfloat16), second.astype(jnp.bfloat16), left_stat_block, right_stat_block)
    results = lax.map(advance, (position_block, square(first_moment), square(second_moment), square(left_statistic), square(right_statistic), square(left_basis), square(right_basis)))
    update, moment, second, left_next, right_next = results
    positions = jnp.take(block_owner, refresh_list).astype(jnp.int32)
    left_frames = square(left_basis)
    right_frames = square(right_basis)
    renewed_left = lax.map(renew_frame, (left_next[positions], left_frames[positions]))
    renewed_right = lax.map(renew_frame, (right_next[positions], right_frames[positions]))
    left_frames = left_frames.at[positions].set(renewed_left)
    right_frames = right_frames.at[positions].set(renewed_right)
    out_shape = first_moment.shape
    return (update.reshape(out_shape), moment.reshape(out_shape), second.reshape(out_shape), left_next.reshape(out_shape), right_next.reshape(out_shape), left_frames.reshape(out_shape), right_frames.reshape(out_shape))
```

```python
import functools
import jax
import jax.numpy as jnp
from jax import lax
from jax.experimental import pallas as pl
from jax.experimental.pallas import tpu as pltpu
from jax.sharding import PartitionSpec as P

BETA_MOMENT = 0.9
BETA_SQUARE = 0.95
BETA_STATS = 0.95
EPSILON = 1e-08
NT = (((1,), (1,)), ((), ()))
NN = (((1,), (0,)), ((), ()))
TN = (((0,), (0,)), ((), ()))


def split(x):
    high = x.astype(jnp.bfloat16)
    low = (x - high.astype(jnp.float32)).astype(jnp.bfloat16)
    return high, low


def dot(a, b, dims):
    return lax.dot_general(a, b, dims, preferred_element_type=jnp.float32)


def dot3(a, b, dims):
    (ah, al), (bh, bl) = a, b
    return dot(ah, bh, dims) + (dot(ah, bl, dims) + dot(al, bh, dims))


def inverse_factor(square, work, side, band=32):
    work[...] = square
    row8 = lax.broadcasted_iota(jnp.int32, (8, side), 0)
    lane8 = lax.broadcasted_iota(jnp.int32, (8, side), 1)
    groups = band // 8
    for start in range(0, side, band):
        rows = [work[start + 8 * q : start + 8 * q + 8, :] for q in range(groups)]
        pivots = []
        for q in range(groups):
            first = start + 8 * q
            cols = [
                [jnp.broadcast_to(rows[r][:, first + j : first + j + 1], (8, side)) for r in range(q, groups)]
                for j in range(8)
            ]
            kept = jnp.ones((8, side), jnp.float32)
            for j in range(8):
                pivot = jnp.broadcast_to(cols[j][0][j : j + 1, :], (8, side))
                kept = jnp.where(row8 == j, pivot, kept)
                inverse = 1.0 / pivot
                scaled = [c * inverse for c in cols[j]]
                scaled[0] = jnp.where(row8 > j, scaled[0], 0.0)
                for k in range(j + 1, 8):
                    lead = jnp.broadcast_to(cols[k][0][j : j + 1, :], (8, side))
                    cols[k] = [c - m * lead for c, m in zip(cols[k], scaled)]
                lead = jnp.broadcast_to(rows[q][j : j + 1, :], (8, side))
                for r in range(q, groups):
                    m = scaled[r - q]
                    mask = lane8 == first + j
                    if r == q:
                        mask = mask & (row8 > j)
                    rows[r] = jnp.where(mask, -m, rows[r] - m * lead)
            pivots.append(kept)
        done = []
        for q in range(groups):
            r = rows[q]
            first = start + 8 * q
            diag = row8 + first
            r = jnp.where(lane8 == diag, 1.0, r) * lax.rsqrt(pivots[q])
            done.append(r)
        panel = jnp.concatenate(done, axis=0)
        rowb = lax.broadcasted_iota(jnp.int32, (band, side), 0) + start
        laneb = lax.broadcasted_iota(jnp.int32, (band, side), 1)
        lower = jnp.where(laneb > rowb, jnp.where(laneb < start + band, 0.0, panel), panel)
        stop = start + band
        if stop < side:
            work[start:stop, :] = jnp.where(laneb > rowb, 0.0, panel)
            rest = side - stop
            upper = jnp.transpose(panel)[stop:, :]
            change = dot3(split(upper), split(lower), NN)
            lane = lax.broadcasted_iota(jnp.int32, (rest, side), 1)
            old = work[stop:, :]
            work[stop:, :] = jnp.where((lane >= start) & (lane < stop), 0.0, old) - change
        else:
            work[start:stop, :] = jnp.where(laneb > rowb, 0.0, panel)
    return work[...]


def frame_kernel(power_ref, own_ref, out_ref, gram, tall, work, *, size, part, side):
    power = power_ref[...]
    for c in range(0, size, 256):
        gram[:, c : c + 256] = dot(power, power[:, c : c + 256], TN)
    tall[...] = own_ref[...].astype(jnp.float32)
    for k in range(0, size, side):
        e = k + side
        inv = inverse_factor(gram[k:e, k:e], work, side)
        invs = split(inv)
        own = dot3(split(tall[:, k:e]), invs, NT)
        out_ref[:, k:e] = own.astype(out_ref.dtype)
        if e < size:
            below = dot3(split(gram[e:, k:e]), invs, NT)
            bh, bl = split(below)
            oh, ol = split(own)
            for c in range(e, size, side):
                lo = c - e
                pair = (bh[lo : lo + side], bl[lo : lo + side])
                gram[c:, c : c + side] = gram[c:, c : c + side] - dot3((bh[lo:], bl[lo:]), pair, NT)
                tall[:, c : c + side] = tall[:, c : c + side] - dot3((oh, ol), pair, NT)


def frame(power, own, side=128):
    size = power.shape[0]
    part = own.shape[0]
    return pl.pallas_call(
        functools.partial(frame_kernel, size=size, part=part, side=side),
        out_shape=jax.ShapeDtypeStruct((part, size), jnp.bfloat16),
        in_specs=[pl.BlockSpec(memory_space=pltpu.VMEM)] * 2,
        out_specs=pl.BlockSpec(memory_space=pltpu.VMEM),
        scratch_shapes=[
            pltpu.VMEM((size, size), jnp.float32),
            pltpu.VMEM((part, size), jnp.float32),
            pltpu.VMEM((side, side), jnp.float32),
        ],
        compiler_params=pltpu.CompilerParams(vmem_limit_bytes=40 * 1024 * 1024),
        cost_estimate=pl.CostEstimate(flops=40 * 10**9, bytes_accessed=4 * 2**20, transcendentals=0),
    )(power, own)


def step_up(i):
    return ((i // 2 + 1) % 4) * 2 + i % 2


def step_down(i):
    return ((i // 2 + 3) % 4) * 2 + i % 2


def step_across(i):
    return ((i // 2 + 2) % 4) * 2 + i % 2


def partner(i):
    return i ^ 1


def send(values, route):
    return lax.ppermute(values, "dp", [(i, route(i)) for i in range(8)])


def ordered(flag, mine, theirs):
    return jnp.where(flag == 0, mine, theirs), jnp.where(flag == 0, theirs, mine)


def body(
    gradient_parts,
    block_owner,
    refresh_list,
    first_moment,
    second_moment,
    left_statistic,
    right_statistic,
    left_basis,
    right_basis,
):
    own_group = lax.axis_index("dp")
    own_lane = lax.axis_index("tensor")
    ring, slot = own_group // 2, own_group % 2
    side, half = ring % 2, ring // 2
    piece = first_moment.shape
    slot_count, _, piece_rows, size = piece
    lanes = 32

    def pick(stacked, index):
        return lax.dynamic_index_in_dim(stacked, index, 0, keepdims=False)

    def paired(values):
        got = send(pick(values, 1 - slot), partner)
        return jnp.concatenate(ordered(slot, pick(values, slot), got), axis=-2)

    def assemble(own, from_up, from_down, from_across):
        whole = jnp.zeros((2, 4) + own.shape[1:], own.dtype)
        for rows, shift in ((own, 0), (from_down, 3), (from_across, 2), (from_up, 1)):
            whole = lax.dynamic_update_slice(
                whole, rows[:, None], (0, (ring + shift) % 4, 0, 0)
            )
        return whole.reshape(size, size)

    def around(pair):
        return assemble(pair, send(pair, step_down), send(pair, step_up), send(pair, step_across))

    def around_sides(pairs, wanted):
        same = jnp.where(wanted == 0, pairs[0], pairs[1])
        other = jnp.where(wanted == 0, pairs[1], pairs[0])
        return assemble(
            same, send(other, step_down), send(other, step_up), send(same, step_across)
        )

    position_block = jnp.argsort(block_owner)
    owned_blocks = lax.dynamic_slice_in_dim(position_block, own_lane * slot_count, slot_count)
    listed = jnp.any(refresh_list[None, :] == owned_blocks[:, None], axis=1)

    with jax.named_scope("sum_groups"):
        parts = lax.all_to_all(
            gradient_parts.reshape(8, piece_rows, 4 * size), "dp", 0, 0, tiled=True
        )
        summed = jnp.sum(parts.astype(jnp.float32), axis=0).astype(jnp.bfloat16)
    summed, left_basis, right_basis, left_wire, right_wire = lax.optimization_barrier(
        (summed, left_basis, right_basis, left_statistic, right_statistic)
    )
    with jax.named_scope("spread"):
        tiles = summed.reshape(4, 16, 4, 8, 128).transpose(0, 3, 2, 1, 4).reshape(lanes, 64, 128)
        spread = lax.all_to_all(tiles, "tensor", 0, 0, tiled=True)
    with jax.named_scope("dispatch"):
        by_block = spread.reshape(16, 2, 4, 16, 128).transpose(0, 2, 1, 3, 4).reshape(64, 32, 128)
        outgoing = jnp.take(by_block, position_block, axis=0).reshape(lanes, 64, 128)
        arrived = lax.all_to_all(outgoing, "tensor", 0, 0, tiled=True)
        owned_grad = (
            arrived.reshape(4, 8, 2, 2, 16, 128).transpose(2, 3, 0, 4, 1, 5).reshape(piece)
        )
    with jax.named_scope("gather_early"):
        stat_pairs = (paired(left_wire), paired(right_wire))
        stat_item = around_sides(stat_pairs, side)
        basis_pairs = (paired(left_basis), paired(right_basis))
        basis_item = around_sides(basis_pairs, side)
        basis_other = around_sides(basis_pairs, 1 - side)
        first_pair = paired(first_moment)
        second_pair = paired(second_moment)
        left_full = jnp.where(side == 0, basis_item, basis_other)
        right_full = jnp.where(side == 0, basis_other, basis_item)
    with jax.named_scope("gather_grad"):
        grad = around(paired(owned_grad))

    with jax.named_scope("products"):
        outer_left = lax.dot_general(
            grad, grad, (((1,), (1,)), ((), ())), preferred_element_type=jnp.float32
        )
        outer_right = lax.dot_general(
            grad, grad, (((0,), (0,)), ((), ())), preferred_element_type=jnp.float32
        )
    with jax.named_scope("power"):
        stat_next = BETA_STATS * stat_item + (1.0 - BETA_STATS) * jnp.where(
            side == 0, outer_left, outer_right
        )
        high = stat_next.astype(jnp.bfloat16)
        low = (stat_next - high.astype(jnp.float32)).astype(jnp.bfloat16)
        power = (
            jnp.dot(high, basis_item, preferred_element_type=jnp.float32)
            + jnp.dot(low, basis_item, preferred_element_type=jnp.float32)
        ).astype(jnp.bfloat16)
        own_power = lax.dynamic_slice_in_dim(power, half * (size // 2), size // 2, 0)
    with jax.named_scope("rotate"):
        group_cols = lax.dynamic_slice_in_dim(
            left_full.reshape(size, 2, size // 2), ring * 128, 128, 2
        )
        turned = jnp.einsum(
            "khc,kn->hcn", group_cols, grad, preferred_element_type=jnp.float32
        ).astype(jnp.bfloat16)
        rotated = jnp.einsum("hcn,nm->hcm", turned, right_full, preferred_element_type=jnp.float32)
        moment = BETA_MOMENT * first_pair.astype(jnp.float32) + (1.0 - BETA_MOMENT) * rotated
        second = (
            BETA_SQUARE * second_pair.astype(jnp.float32)
            + (1.0 - BETA_SQUARE) * rotated * rotated
        )
        direction = (moment / (jnp.sqrt(second) + EPSILON)).astype(jnp.bfloat16)
        returned = jnp.einsum(
            "hcm,nm->hcn", direction, right_full, preferred_element_type=jnp.float32
        ).astype(jnp.bfloat16)
        returned_full = around(returned)

    def ring_rows(matrix):
        rows = matrix.reshape(2, 4, 2 * piece_rows, size)
        return lax.dynamic_index_in_dim(rows, ring, 1, keepdims=False)

    def unpaired(rows):
        by_partner = rows.reshape(2, 2, piece_rows, size).swapaxes(0, 1)
        got = send(pick(by_partner, 1 - slot), partner)
        return jnp.stack(ordered(slot, pick(by_partner, slot), got))

    with jax.named_scope("statistics"):
        left_next = BETA_STATS * left_statistic + (1.0 - BETA_STATS) * unpaired(
            ring_rows(outer_left)
        )
        right_next = BETA_STATS * right_statistic + (1.0 - BETA_STATS) * unpaired(
            ring_rows(outer_right)
        )
    with jax.named_scope("frame"):
        framed = frame(power, own_power)
        back = lax.all_to_all(
            framed.reshape(8, piece_rows, size), "dp", 0, 0, tiled=True
        ).reshape(2, 2, 2, piece_rows, size)
    with jax.named_scope("update"):
        update = unpaired(
            jnp.einsum(
                "hck,kn->hcn",
                ring_rows(left_full),
                returned_full,
                preferred_element_type=jnp.float32,
            ).astype(jnp.bfloat16)
        )
        moment_next = unpaired(moment.astype(jnp.bfloat16))
        second_next = unpaired(second.astype(jnp.bfloat16))
    with jax.named_scope("renew"):
        marker = listed[:, None, None, None]
        renewed = back.transpose(1, 2, 0, 3, 4)
        left_basis_next = jnp.where(marker, renewed[0], left_basis)
        right_basis_next = jnp.where(marker, renewed[1], right_basis)
    return (
        update,
        moment_next,
        second_next,
        left_next,
        right_next,
        left_basis_next,
        right_basis_next,
    )


def solution(mesh):
    held = P("tensor", None, "dp", None)
    in_specs = (P("dp", "tensor", None), P(), P()) + (held,) * 6
    out_specs = (held,) * 7
    return jax.shard_map(body, mesh=mesh, in_specs=in_specs, out_specs=out_specs, check_vma=False)
```

```python
import functools
import jax
import jax.numpy as jnp
from jax import lax
from jax.experimental import pallas as pl
from jax.experimental.pallas import tpu as pltpu
from jax.sharding import PartitionSpec as P

BETA_MOMENT = 0.9
BETA_SQUARE = 0.95
BETA_STATS = 0.95
EPSILON = 1e-08
NT = (((1,), (1,)), ((), ()))
NN = (((1,), (0,)), ((), ()))
TN = (((0,), (0,)), ((), ()))


def split(x):
    high = x.astype(jnp.bfloat16)
    low = (x - high.astype(jnp.float32)).astype(jnp.bfloat16)
    return high, low


def dot(a, b, dims):
    return lax.dot_general(a, b, dims, preferred_element_type=jnp.float32)


def dot3(a, b, dims):
    (ah, al), (bh, bl) = a, b
    return dot(ah, bh, dims) + (dot(ah, bl, dims) + dot(al, bh, dims))


def inverse_factor(square, work, side, band=32):
    work[...] = square
    row8 = lax.broadcasted_iota(jnp.int32, (8, side), 0)
    lane8 = lax.broadcasted_iota(jnp.int32, (8, side), 1)
    groups = band // 8
    for start in range(0, side, band):
        rows = [work[start + 8 * q : start + 8 * q + 8, :] for q in range(groups)]
        pivots = []
        for q in range(groups):
            first = start + 8 * q
            cols = [
                [jnp.broadcast_to(rows[r][:, first + j : first + j + 1], (8, side)) for r in range(q, groups)]
                for j in range(8)
            ]
            kept = jnp.ones((8, side), jnp.float32)
            for j in range(8):
                pivot = jnp.broadcast_to(cols[j][0][j : j + 1, :], (8, side))
                kept = jnp.where(row8 == j, pivot, kept)
                inverse = 1.0 / pivot
                scaled = [c * inverse for c in cols[j]]
                scaled[0] = jnp.where(row8 > j, scaled[0], 0.0)
                for k in range(j + 1, 8):
                    lead = jnp.broadcast_to(cols[k][0][j : j + 1, :], (8, side))
                    cols[k] = [c - m * lead for c, m in zip(cols[k], scaled)]
                lead = jnp.broadcast_to(rows[q][j : j + 1, :], (8, side))
                for r in range(q, groups):
                    m = scaled[r - q]
                    mask = lane8 == first + j
                    if r == q:
                        mask = mask & (row8 > j)
                    rows[r] = jnp.where(mask, -m, rows[r] - m * lead)
            pivots.append(kept)
        done = []
        for q in range(groups):
            r = rows[q]
            first = start + 8 * q
            diag = row8 + first
            r = jnp.where(lane8 == diag, 1.0, r) * lax.rsqrt(pivots[q])
            done.append(r)
        panel = jnp.concatenate(done, axis=0)
        rowb = lax.broadcasted_iota(jnp.int32, (band, side), 0) + start
        laneb = lax.broadcasted_iota(jnp.int32, (band, side), 1)
        lower = jnp.where(laneb > rowb, jnp.where(laneb < start + band, 0.0, panel), panel)
        stop = start + band
        if stop < side:
            work[start:stop, :] = jnp.where(laneb > rowb, 0.0, panel)
            rest = side - stop
            upper = jnp.transpose(panel)[stop:, :]
            change = dot3(split(upper), split(lower), NN)
            lane = lax.broadcasted_iota(jnp.int32, (rest, side), 1)
            old = work[stop:, :]
            work[stop:, :] = jnp.where((lane >= start) & (lane < stop), 0.0, old) - change
        else:
            work[start:stop, :] = jnp.where(laneb > rowb, 0.0, panel)
    return work[...]


def vmem(count):
    return [pl.BlockSpec(memory_space=pltpu.VMEM)] * count


SMEM = pl.BlockSpec(memory_space=pltpu.SMEM)
PARAMS = pltpu.CompilerParams(vmem_limit_bytes=48 * 1024 * 1024)


def cost(flops, size):
    return pl.CostEstimate(flops=flops, bytes_accessed=size, transcendentals=0)


def place(pieces, ring, whole):
    for piece, shift in zip(pieces, (0, 3, 2, 1)):
        at = lax.rem(ring + shift, 4) * 128
        for h in range(2):
            whole[pl.ds(pl.multiple_of(h * 512 + at, 128), 128), :] = piece[h]


def statistic_kernel(info, a0, a1, a2, a3, out_ref, basis_ref, stat):
    ring = info[0]
    pieces = (a0, a1, a2, a3)
    place([p.at[0] for p in pieces], ring, stat)
    place([p.at[1] for p in pieces], ring, basis_ref)
    basis = basis_ref[...]
    for r in range(0, 1024, 256):
        out_ref[r : r + 256, :] = dot(stat[r : r + 256, :], basis, NN)


def statistic_times_basis(info, pieces):
    return pl.pallas_call(
        statistic_kernel,
        out_shape=(
            jax.ShapeDtypeStruct((1024, 1024), jnp.float32),
            jax.ShapeDtypeStruct((1024, 1024), jnp.bfloat16),
        ),
        grid=(1,),
        in_specs=[SMEM] + [pl.BlockSpec((2, 2, 128, 1024), lambda i: (0, 0, 0, 0))] * 4,
        out_specs=tuple(vmem(2)),
        scratch_shapes=[pltpu.VMEM((1024, 1024), jnp.bfloat16)],
        compiler_params=PARAMS,
        cost_estimate=cost(2 * 1024**3, 10 * 2**20),
    )(info, *pieces)


def rotate_kernel(
    info, g0, g1, g2, g3, item, o0, o1, o2, o3, first, second,
    grad, returned, keep16, keep32, wire, other, lhs, step,
):
    ring, slot, side = info[0], info[1], info[2]
    place((g0, g1, g2, g3), ring, grad)
    place([p.at[0] for p in (o0, o1, o2, o3)], ring, other)
    whole = grad[...]

    def divide(rows, h, keep, index, place_on_wire):
        low, high = rows[:64], rows[64:]
        keep[index, h] = jnp.where(slot == 0, low, high).astype(keep.dtype)
        wire[place_on_wire, h] = jnp.where(slot == 0, high, low).astype(wire.dtype)

    def run(left, right):
        for h in range(2):
            at = pl.multiple_of(h * 512 + ring * 128, 128)
            lhs[h * 128 : h * 128 + 128, :] = dot(left[:, pl.ds(at, 128)], whole, TN).astype(
                jnp.bfloat16
            )
        step[...] = dot(lhs[...], right[...], NN)
        for h in range(2):
            rotated = step[h * 128 : h * 128 + 128, :]
            moment = BETA_MOMENT * first[h].astype(jnp.float32) + (1.0 - BETA_MOMENT) * rotated
            square = (
                BETA_SQUARE * second[h].astype(jnp.float32)
                + (1.0 - BETA_SQUARE) * rotated * rotated
            )
            divide(moment, h, keep16, 0, 0)
            divide(square, h, keep16, 1, 1)
            lhs[h * 128 : h * 128 + 128, :] = (moment / (jnp.sqrt(square) + EPSILON)).astype(
                jnp.bfloat16
            )
        back = dot(lhs[...], right[...], NT)
        for h in range(2):
            returned[h] = back[h * 128 : h * 128 + 128].astype(jnp.bfloat16)

    @pl.when(side == 0)
    def _():
        run(item, other)

    @pl.when(side == 1)
    def _():
        run(other, item)

    for h in range(2):
        at = pl.multiple_of(h * 512 + ring * 128, 128)
        divide(dot(grad[pl.ds(at, 128), :], whole, NT), h, keep32, 0, 2)
        divide(dot(grad[:, pl.ds(at, 128)], whole, TN), h, keep32, 1, 3)


def rotate(info, grad_pieces, item, other_pieces, first, second):
    shape = jax.ShapeDtypeStruct
    return pl.pallas_call(
        rotate_kernel,
        out_shape=(
            shape((1024, 1024), jnp.bfloat16),
            shape((2, 128, 1024), jnp.bfloat16),
            shape((2, 2, 64, 1024), jnp.bfloat16),
            shape((2, 2, 64, 1024), jnp.float32),
            shape((4, 2, 64, 1024), jnp.bfloat16),
        ),
        grid=(1,),
        in_specs=[SMEM]
        + vmem(5)
        + [pl.BlockSpec((1, 2, 128, 1024), lambda i: (2, 0, 0, 0))] * 4
        + vmem(2),
        out_specs=tuple(vmem(5)),
        scratch_shapes=[
            pltpu.VMEM((1024, 1024), jnp.bfloat16),
            pltpu.VMEM((256, 1024), jnp.bfloat16),
            pltpu.VMEM((256, 1024), jnp.float32),
        ],
        compiler_params=PARAMS,
        cost_estimate=cost(5 * 512 * 1024**2, 13 * 2**20),
    )(info, *grad_pieces, item, *other_pieces, first, second)


def update_kernel(info, rows, r0, r1, r2, r3, keep, wire, whole):
    ring, slot = info[0], info[1]
    place((r0, r1, r2, r3), ring, whole)
    for h in range(2):
        out = dot(rows[h], whole[...], NN)
        low, high = out[:64], out[64:]
        keep[h] = jnp.where(slot == 0, low, high).astype(keep.dtype)
        wire[h] = jnp.where(slot == 0, high, low).astype(wire.dtype)


def update_rows(info, rows, pieces):
    shape = jax.ShapeDtypeStruct((2, 64, 1024), jnp.bfloat16)
    return pl.pallas_call(
        update_kernel,
        out_shape=(shape, shape),
        in_specs=[SMEM] + vmem(5),
        out_specs=tuple(vmem(2)),
        scratch_shapes=[pltpu.VMEM((1024, 1024), jnp.bfloat16)],
        compiler_params=PARAMS,
        cost_estimate=cost(512 * 1024**2, 4 * 2**20),
    )(info, rows, *pieces)


def frame_kernel(info, grad, basis, early, out_ref, gram, tall, work, outer, power, *, side):
    size, part = gram.shape[0], tall.shape[0]

    @pl.when(info[2] == 0)
    def _():
        for c in range(0, size, 256):
            outer[c : c + 256, :] = dot(grad[c : c + 256, :], grad[...], NT).astype(jnp.bfloat16)

    @pl.when(info[2] == 1)
    def _():
        for c in range(0, size, 256):
            outer[c : c + 256, :] = dot(grad[:, c : c + 256], grad[...], TN).astype(jnp.bfloat16)

    for c in range(0, size, 256):
        power[c : c + 256, :] = (
            BETA_STATS * early[c : c + 256, :]
            + (1.0 - BETA_STATS) * dot(outer[c : c + 256, :], basis[...], NN)
        ).astype(jnp.bfloat16)
    for c in range(0, size, 256):
        gram[c:, c : c + 256] = dot(power[:, c:], power[:, c : c + 256], TN)
    tall[...] = power[pl.ds(pl.multiple_of(info[3] * part, part), part), :].astype(jnp.float32)
    for k in range(0, size, side):
        e = k + side
        inv = inverse_factor(gram[k:e, k:e], work, side)
        invs = split(inv)
        own = dot3(split(tall[:, k:e]), invs, NT)
        out_ref[:, k:e] = own.astype(out_ref.dtype)
        if e < size:
            below = dot3(split(gram[e:, k:e]), invs, NT)
            bh, bl = split(below)
            oh, ol = split(own)
            for c in range(e, size, side):
                lo = c - e
                pair = (bh[lo : lo + side], bl[lo : lo + side])
                gram[c:, c : c + side] = gram[c:, c : c + side] - dot3((bh[lo:], bl[lo:]), pair, NT)
                tall[:, c : c + side] = tall[:, c : c + side] - dot3((oh, ol), pair, NT)


def frame(info, grad, basis, early, side=128):
    size = grad.shape[0]
    part = size // 2
    return pl.pallas_call(
        functools.partial(frame_kernel, side=side),
        out_shape=jax.ShapeDtypeStruct((part, size), jnp.bfloat16),
        in_specs=[SMEM] + vmem(3),
        out_specs=pl.BlockSpec(memory_space=pltpu.VMEM),
        scratch_shapes=[
            pltpu.VMEM((size, size), jnp.float32),
            pltpu.VMEM((part, size), jnp.float32),
            pltpu.VMEM((side, side), jnp.float32),
            pltpu.VMEM((size, size), jnp.bfloat16),
            pltpu.VMEM((size, size), jnp.bfloat16),
        ],
        compiler_params=PARAMS,
        cost_estimate=cost(50 * 10**9, 9 * 2**20),
    )(info, grad, basis, early)


def step_up(i):
    return ((i // 2 + 1) % 4) * 2 + i % 2


def step_down(i):
    return ((i // 2 + 3) % 4) * 2 + i % 2


def step_across(i):
    return ((i // 2 + 2) % 4) * 2 + i % 2


def partner(i):
    return i ^ 1


def send(values, route):
    return lax.ppermute(values, "dp", [(i, route(i)) for i in range(8)])


def ordered(flag, mine, theirs):
    return jnp.where(flag == 0, mine, theirs), jnp.where(flag == 0, theirs, mine)


def pick(stacked, index):
    return lax.dynamic_index_in_dim(stacked, index, 0, keepdims=False)


tie = lax.optimization_barrier


def body(
    gradient_parts,
    block_owner,
    refresh_list,
    first_moment,
    second_moment,
    left_statistic,
    right_statistic,
    left_basis,
    right_basis,
):
    own_group = lax.axis_index("dp")
    own_lane = lax.axis_index("tensor")
    ring, slot = own_group // 2, own_group % 2
    side, half = ring % 2, ring // 2
    info = jnp.stack([ring, slot, side, half]).astype(jnp.int32)
    piece = first_moment.shape
    slot_count, _, piece_rows, size = piece
    lanes = 32

    def around(pair):
        return pair, send(pair, step_up), send(pair, step_across), send(pair, step_down)

    position_block = jnp.argsort(block_owner)
    owned_blocks = lax.dynamic_slice_in_dim(position_block, own_lane * slot_count, slot_count)
    listed = jnp.any(refresh_list[None, :] == owned_blocks[:, None], axis=1)

    with jax.named_scope("sum_groups"):
        chunks = gradient_parts.reshape(4, 2, piece_rows, 4 * size)

        def chunk(shift):
            return pick(chunks, (ring + shift) % 4)

        wide = (2 * piece_rows, 4 * size)
        opposite = chunk(2)
        from_partner = send(pick(opposite, 1 - slot), partner)
        from_down = send(chunk(1).reshape(wide), step_up)
        from_up = send(chunk(3).reshape(wide), step_down)
        halfway = from_partner.astype(jnp.float32) + pick(opposite, slot).astype(jnp.float32)
        from_across = send(halfway.astype(jnp.bfloat16), step_across)
        near = (
            from_down.astype(jnp.float32)
            + from_up.astype(jnp.float32)
            + chunk(0).reshape(wide).astype(jnp.float32)
        ).reshape(2, piece_rows, 4 * size)
        to_next = pick(near, 1 - slot).astype(jnp.bfloat16)
        from_next = send(to_next, partner)
        summed = (
            pick(near, slot) + from_next.astype(jnp.float32) + from_across.astype(jnp.float32)
        ).astype(jnp.bfloat16)

    with jax.named_scope("early_partner"):
        slot_major = jnp.stack(
            [
                left_statistic.astype(jnp.bfloat16),
                right_statistic.astype(jnp.bfloat16),
                left_basis,
                right_basis,
            ],
            axis=1,
        )
        outgoing, _ = tie((pick(slot_major, 1 - slot), from_partner))
        got = send(outgoing, partner)
        early = jnp.concatenate(ordered(slot, pick(slot_major, slot), got), axis=-2)
        left_rows = early[2]
    lefts, rights = early[0::2], early[1::2]
    same = jnp.where(side == 0, lefts, rights)
    cross = jnp.where(side == 0, rights, lefts)
    same = jnp.concatenate([same, cross[1:]])
    cross = jnp.concatenate([cross, same[1:2]])

    with jax.named_scope("spread"):
        tiles = summed.reshape(4, 16, 4, 8, 128).transpose(0, 3, 2, 1, 4).reshape(lanes, 64, 128)
        spread = lax.all_to_all(tiles, "tensor", 0, 0, tiled=True)
    with jax.named_scope("early_near"):
        cross, _ = tie((cross, to_next))
        item_up, item_down = send(cross, step_up), send(cross, step_down)
        moments, _ = tie((jnp.stack([first_moment, second_moment], axis=1), summed))
        got_moments = send(pick(moments, 1 - slot), partner)
    with jax.named_scope("dispatch"):
        by_block = spread.reshape(16, 2, 4, 16, 128).transpose(0, 2, 1, 3, 4).reshape(64, 32, 128)
        routed = by_block.at[position_block].get(mode="promise_in_bounds").reshape(lanes, 64, 128)
        same_tied, item_up, item_down, routed = tie((same, item_up, item_down, routed))
        arrived = lax.all_to_all(routed, "tensor", 0, 0, tiled=True)
    with jax.named_scope("early_far"):
        item_across = send(same_tied, step_across)
        item_pieces = (same, item_up, item_across, item_down)
    with jax.named_scope("gather_grad"):
        by_slot = arrived.reshape(4, 8, 2, 2, 16, 128).transpose(2, 3, 0, 4, 1, 5).reshape(piece)
        got_grad = send(pick(by_slot, 1 - slot), partner)
        item_pieces, got_grad = tie((item_pieces, got_grad))
        grad_pieces = around(
            jnp.concatenate(ordered(slot, pick(by_slot, slot), got_grad), axis=-2)
        )
    with jax.named_scope("early_product"):
        early_power, item = statistic_times_basis(info, item_pieces)
        moment_rows = jnp.concatenate(
            ordered(slot, pick(moments, slot), got_moments), axis=-2
        )
    with jax.named_scope("rotate"):
        grad, returned, keep16, keep32, wire = rotate(
            info, grad_pieces, item, item_pieces, moment_rows[0], moment_rows[1]
        )
    with jax.named_scope("exchange"):
        returned_pieces = around(returned)
        got = send(wire, partner)
    with jax.named_scope("frame"):
        framed = frame(info, grad, item, early_power)
        framed, returned_pieces = tie((framed, returned_pieces))
        back = lax.all_to_all(
            framed.reshape(8, piece_rows, size), "dp", 0, 0, tiled=True
        ).reshape(2, 2, 2, piece_rows, size)
    with jax.named_scope("update"):
        mine, theirs = update_rows(info, left_rows, returned_pieces)
        update = jnp.stack(ordered(slot, mine, send(theirs, partner)))
        moment_next = jnp.stack(ordered(slot, keep16[0], got[0]))
        second_next = jnp.stack(ordered(slot, keep16[1], got[1]))

        def statistic_next(statistic, kept, came):
            outer = jnp.stack(ordered(slot, kept, came.astype(jnp.float32)))
            return BETA_STATS * statistic + (1.0 - BETA_STATS) * outer

        left_next = statistic_next(left_statistic, keep32[0], got[2])
        right_next = statistic_next(right_statistic, keep32[1], got[3])
    with jax.named_scope("renew"):
        marker = listed[:, None, None, None]
        renewed = back.transpose(1, 2, 0, 3, 4)
        left_basis_next = jnp.where(marker, renewed[0], left_basis)
        right_basis_next = jnp.where(marker, renewed[1], right_basis)
    return (
        update,
        moment_next,
        second_next,
        left_next,
        right_next,
        left_basis_next,
        right_basis_next,
    )


def solution(mesh):
    held = P("tensor", None, "dp", None)
    in_specs = (P("dp", "tensor", None), P(), P()) + (held,) * 6
    out_specs = (held,) * 7
    return jax.shard_map(body, mesh=mesh, in_specs=in_specs, out_specs=out_specs, check_vma=False)
```

```python
import functools
import jax
import jax.numpy as jnp
from jax import lax
from jax.experimental import pallas as pl
from jax.experimental.pallas import tpu as pltpu
from jax.sharding import PartitionSpec as P

BETA_MOMENT = 0.9
BETA_SQUARE = 0.95
BETA_STATS = 0.95
EPSILON = 1e-08
NT = (((1,), (1,)), ((), ()))
NN = (((1,), (0,)), ((), ()))
TN = (((0,), (0,)), ((), ()))


def split(x):
    high = x.astype(jnp.bfloat16)
    low = (x - high.astype(jnp.float32)).astype(jnp.bfloat16)
    return high, low


def dot(a, b, dims):
    return lax.dot_general(a, b, dims, preferred_element_type=jnp.float32)


def dot3(a, b, dims):
    (ah, al), (bh, bl) = a, b
    return dot(ah, bh, dims) + (dot(ah, bl, dims) + dot(al, bh, dims))


def inverse_factor(square, work, side, band=32):
    work[...] = square
    row8 = lax.broadcasted_iota(jnp.int32, (8, side), 0)
    lane8 = lax.broadcasted_iota(jnp.int32, (8, side), 1)
    groups = band // 8
    for start in range(0, side, band):
        rows = [work[start + 8 * q : start + 8 * q + 8, :] for q in range(groups)]
        pivots = []
        for q in range(groups):
            first = start + 8 * q
            cols = [
                [jnp.broadcast_to(rows[r][:, first + j : first + j + 1], (8, side)) for r in range(q, groups)]
                for j in range(8)
            ]
            kept = jnp.ones((8, side), jnp.float32)
            for j in range(8):
                pivot = jnp.broadcast_to(cols[j][0][j : j + 1, :], (8, side))
                kept = jnp.where(row8 == j, pivot, kept)
                inverse = 1.0 / pivot
                scaled = [c * inverse for c in cols[j]]
                scaled[0] = jnp.where(row8 > j, scaled[0], 0.0)
                for k in range(j + 1, 8):
                    lead = jnp.broadcast_to(cols[k][0][j : j + 1, :], (8, side))
                    cols[k] = [c - m * lead for c, m in zip(cols[k], scaled)]
                lead = jnp.broadcast_to(rows[q][j : j + 1, :], (8, side))
                for r in range(q, groups):
                    m = scaled[r - q]
                    mask = lane8 == first + j
                    if r == q:
                        mask = mask & (row8 > j)
                    rows[r] = jnp.where(mask, -m, rows[r] - m * lead)
            pivots.append(kept)
        done = []
        for q in range(groups):
            r = rows[q]
            first = start + 8 * q
            diag = row8 + first
            r = jnp.where(lane8 == diag, 1.0, r) * lax.rsqrt(pivots[q])
            done.append(r)
        panel = jnp.concatenate(done, axis=0)
        rowb = lax.broadcasted_iota(jnp.int32, (band, side), 0) + start
        laneb = lax.broadcasted_iota(jnp.int32, (band, side), 1)
        lower = jnp.where(laneb > rowb, jnp.where(laneb < start + band, 0.0, panel), panel)
        stop = start + band
        if stop < side:
            work[start:stop, :] = jnp.where(laneb > rowb, 0.0, panel)
            rest = side - stop
            upper = jnp.transpose(panel)[stop:, :]
            change = dot3(split(upper), split(lower), NN)
            lane = lax.broadcasted_iota(jnp.int32, (rest, side), 1)
            old = work[stop:, :]
            work[stop:, :] = jnp.where((lane >= start) & (lane < stop), 0.0, old) - change
        else:
            work[start:stop, :] = jnp.where(laneb > rowb, 0.0, panel)
    return work[...]


def vmem(count):
    return [pl.BlockSpec(memory_space=pltpu.VMEM)] * count


SMEM = pl.BlockSpec(memory_space=pltpu.SMEM)
PARAMS = pltpu.CompilerParams(vmem_limit_bytes=48 * 1024 * 1024)


def cost(flops, size):
    return pl.CostEstimate(flops=flops, bytes_accessed=size, transcendentals=0)


def place(pieces, ring, whole, first=0, count=128):
    for piece, shift in zip(pieces, (0, 3, 2, 1)):
        at = lax.rem(ring + shift, 4) * 128 + first
        for h in range(2):
            whole[pl.ds(pl.multiple_of(h * 512 + at, 64), count), :] = piece[h][...]


def statistic_kernel(info, a0, a1, a2, a3, out_ref, basis_ref, stat):
    ring = info[0]
    pieces = (a0, a1, a2, a3)
    place([p.at[0] for p in pieces], ring, stat)
    place([p.at[1] for p in pieces], ring, basis_ref)
    basis = basis_ref[...]
    for r in range(0, 1024, 256):
        out_ref[r : r + 256, :] = dot(stat[r : r + 256, :], basis, NN)


def statistic_times_basis(info, pieces):
    return pl.pallas_call(
        statistic_kernel,
        out_shape=(
            jax.ShapeDtypeStruct((1024, 1024), jnp.float32),
            jax.ShapeDtypeStruct((1024, 1024), jnp.bfloat16),
        ),
        in_specs=[SMEM] + vmem(4),
        out_specs=tuple(vmem(2)),
        scratch_shapes=[pltpu.VMEM((1024, 1024), jnp.bfloat16)],
        compiler_params=PARAMS,
        cost_estimate=cost(2 * 1024**3, 10 * 2**20),
    )(info, *pieces)


def rotate_kernel(
    info, grad, item, o0, o1, o2, o3, first, second,
    returned, keep16, keep32, wire, other, lhs, step,
):
    ring, slot, side = info[0], info[1], info[2]
    place((o0, o1, o2, o3), ring, other)
    whole = grad[...]

    def divide(rows, h, keep, index, place_on_wire):
        low, high = rows[:64], rows[64:]
        keep[index, h] = jnp.where(slot == 0, low, high).astype(keep.dtype)
        wire[place_on_wire, h] = jnp.where(slot == 0, high, low).astype(wire.dtype)

    def run(left, right):
        for h in range(2):
            at = pl.multiple_of(h * 512 + ring * 128, 128)
            lhs[h * 128 : h * 128 + 128, :] = dot(left[:, pl.ds(at, 128)], whole, TN).astype(
                jnp.bfloat16
            )
        step[...] = dot(lhs[...], right[...], NN)
        for h in range(2):
            rotated = step[h * 128 : h * 128 + 128, :]
            moment = BETA_MOMENT * first[h].astype(jnp.float32) + (1.0 - BETA_MOMENT) * rotated
            square = (
                BETA_SQUARE * second[h].astype(jnp.float32)
                + (1.0 - BETA_SQUARE) * rotated * rotated
            )
            divide(moment, h, keep16, 0, 0)
            divide(square, h, keep16, 1, 1)
            lhs[h * 128 : h * 128 + 128, :] = (moment / (jnp.sqrt(square) + EPSILON)).astype(
                jnp.bfloat16
            )
        back = dot(lhs[...], right[...], NT)
        for h in range(2):
            returned[h] = back[h * 128 : h * 128 + 128].astype(jnp.bfloat16)

    @pl.when(side == 0)
    def _():
        run(item, other)

    @pl.when(side == 1)
    def _():
        run(other, item)

    for h in range(2):
        at = pl.multiple_of(h * 512 + ring * 128, 128)
        divide(dot(grad[pl.ds(at, 128), :], whole, NT), h, keep32, 0, 2)
        divide(dot(grad[:, pl.ds(at, 128)], whole, TN), h, keep32, 1, 3)


def rotate(info, grad, item, other_pieces, first, second):
    shape = jax.ShapeDtypeStruct
    return pl.pallas_call(
        rotate_kernel,
        out_shape=(
            shape((2, 128, 1024), jnp.bfloat16),
            shape((2, 2, 64, 1024), jnp.bfloat16),
            shape((2, 2, 64, 1024), jnp.float32),
            shape((4, 2, 64, 1024), jnp.bfloat16),
        ),
        in_specs=[SMEM] + vmem(8),
        out_specs=tuple(vmem(4)),
        scratch_shapes=[
            pltpu.VMEM((1024, 1024), jnp.bfloat16),
            pltpu.VMEM((256, 1024), jnp.bfloat16),
            pltpu.VMEM((256, 1024), jnp.float32),
        ],
        compiler_params=PARAMS,
        cost_estimate=cost(5 * 512 * 1024**2, 13 * 2**20),
    )(info, grad, item, *other_pieces, first, second)


def update_kernel(info, rows, whole, keep, wire):
    slot = info[1]
    for h in range(2):
        out = dot(rows[h], whole[...], NN)
        low, high = out[:64], out[64:]
        keep[h] = jnp.where(slot == 0, low, high).astype(keep.dtype)
        wire[h] = jnp.where(slot == 0, high, low).astype(wire.dtype)


def update_rows(info, rows, whole):
    shape = jax.ShapeDtypeStruct((2, 64, 1024), jnp.bfloat16)
    return pl.pallas_call(
        update_kernel,
        out_shape=(shape, shape),
        in_specs=[SMEM] + vmem(2),
        out_specs=tuple(vmem(2)),
        compiler_params=PARAMS,
        cost_estimate=cost(512 * 1024**2, 4 * 2**20),
    )(info, rows, whole)


def eliminate(gram, tall, work, out_ref, stop, side):
    size = gram.shape[0]
    for k in range(0, stop, side):
        e = k + side
        inv = inverse_factor(gram[k:e, k:e], work, side)
        invs = split(inv)
        own = dot3(split(tall[:, k:e]), invs, NT)
        out_ref[:, k:e] = own.astype(out_ref.dtype)
        if e < size:
            below = dot3(split(gram[e:, k:e]), invs, NT)
            bh, bl = split(below)
            oh, ol = split(own)
            for c in range(e, size, side):
                lo = c - e
                pair = (bh[lo : lo + side], bl[lo : lo + side])
                gram[c:, c : c + side] = gram[c:, c : c + side] - dot3((bh[lo:], bl[lo:]), pair, NT)
                tall[:, c : c + side] = tall[:, c : c + side] - dot3((oh, ol), pair, NT)


def frame_first_kernel(
    info, m0, m1, m2, m3, t0, t1, t2, t3, basis, early,
    grad, out_ref, gram_rest, tall_rest, gram, tall, work, outer, power, *, side,
):
    size, part = gram.shape[0], tall.shape[0]
    stop = out_ref.shape[1]
    ring, slot = info[0], info[1]
    place((m0, m1, m2, m3), ring, grad, slot * 64, 64)
    place((t0, t1, t2, t3), ring, grad, (1 - slot) * 64, 64)

    @pl.when(info[2] == 0)
    def _():
        for c in range(0, size, 256):
            outer[c : c + 256, :] = dot(grad[c : c + 256, :], grad[...], NT).astype(jnp.bfloat16)

    @pl.when(info[2] == 1)
    def _():
        for c in range(0, size, 256):
            outer[c : c + 256, :] = dot(grad[:, c : c + 256], grad[...], TN).astype(jnp.bfloat16)

    for c in range(0, size, 256):
        power[c : c + 256, :] = (
            BETA_STATS * early[c : c + 256, :]
            + (1.0 - BETA_STATS) * dot(outer[c : c + 256, :], basis[...], NN)
        ).astype(jnp.bfloat16)
    for c in range(0, size, 256):
        gram[c:, c : c + 256] = dot(power[:, c:], power[:, c : c + 256], TN)
    tall[...] = power[pl.ds(pl.multiple_of(info[3] * part, part), part), :].astype(jnp.float32)
    eliminate(gram, tall, work, out_ref, stop, side)
    gram_rest[...] = gram[stop:, stop:]
    tall_rest[...] = tall[:, stop:]


def frame_first(info, grad_pieces, basis, early, stop=512, side=128):
    size = basis.shape[0]
    part = size // 2
    shape = jax.ShapeDtypeStruct
    return pl.pallas_call(
        functools.partial(frame_first_kernel, side=side),
        out_shape=(
            shape((size, size), jnp.bfloat16),
            shape((part, stop), jnp.bfloat16),
            shape((size - stop, size - stop), jnp.float32),
            shape((part, size - stop), jnp.float32),
        ),
        in_specs=[SMEM] + vmem(10),
        out_specs=tuple(vmem(4)),
        scratch_shapes=[
            pltpu.VMEM((size, size), jnp.float32),
            pltpu.VMEM((part, size), jnp.float32),
            pltpu.VMEM((side, side), jnp.float32),
            pltpu.VMEM((size, size), jnp.bfloat16),
            pltpu.VMEM((size, size), jnp.bfloat16),
        ],
        compiler_params=PARAMS,
        cost_estimate=cost(30 * 10**9, 12 * 2**20),
    )(info, *grad_pieces, basis, early)


def frame_second_kernel(gram_rest, tall_rest, out_ref, gram, tall, work, *, side):
    gram[...] = gram_rest[...]
    tall[...] = tall_rest[...]
    eliminate(gram, tall, work, out_ref, gram.shape[0], side)


def frame_second(gram_rest, tall_rest, side=128):
    return pl.pallas_call(
        functools.partial(frame_second_kernel, side=side),
        out_shape=jax.ShapeDtypeStruct(tall_rest.shape, jnp.bfloat16),
        in_specs=vmem(2),
        out_specs=pl.BlockSpec(memory_space=pltpu.VMEM),
        scratch_shapes=[
            pltpu.VMEM(gram_rest.shape, jnp.float32),
            pltpu.VMEM(tall_rest.shape, jnp.float32),
            pltpu.VMEM((side, side), jnp.float32),
        ],
        compiler_params=PARAMS,
        cost_estimate=cost(20 * 10**9, 3 * 2**20),
    )(gram_rest, tall_rest)


def step_up(i):
    return ((i // 2 + 1) % 4) * 2 + i % 2


def step_down(i):
    return ((i // 2 + 3) % 4) * 2 + i % 2


def step_across(i):
    return ((i // 2 + 2) % 4) * 2 + i % 2


def partner(i):
    return i ^ 1


def send(values, route):
    return lax.ppermute(values, "dp", [(i, route(i)) for i in range(8)])


def ordered(flag, mine, theirs):
    return jnp.where(flag == 0, mine, theirs), jnp.where(flag == 0, theirs, mine)


def pick(stacked, index):
    return lax.dynamic_index_in_dim(stacked, index, 0, keepdims=False)


tie = lax.optimization_barrier


def body(
    gradient_parts,
    block_owner,
    refresh_list,
    first_moment,
    second_moment,
    left_statistic,
    right_statistic,
    left_basis,
    right_basis,
):
    own_group = lax.axis_index("dp")
    own_lane = lax.axis_index("tensor")
    ring, slot = own_group // 2, own_group % 2
    side, half = ring % 2, ring // 2
    info = jnp.stack([ring, slot, side, half]).astype(jnp.int32)
    piece = first_moment.shape
    slot_count, _, piece_rows, size = piece
    lanes = 32

    def around(pair):
        return pair, send(pair, step_up), send(pair, step_across), send(pair, step_down)

    position_block = jnp.argsort(block_owner)
    owned_blocks = lax.dynamic_slice_in_dim(position_block, own_lane * slot_count, slot_count)
    listed = jnp.any(refresh_list[None, :] == owned_blocks[:, None], axis=1)

    with jax.named_scope("sum_groups"):
        chunks = gradient_parts.reshape(4, 2, piece_rows, 4 * size)

        def chunk(shift):
            return pick(chunks, (ring + shift) % 4)

        wide = (2 * piece_rows, 4 * size)
        opposite = chunk(2)
        from_partner = send(pick(opposite, 1 - slot), partner)
        from_down = send(chunk(1).reshape(wide), step_up)
        from_up = send(chunk(3).reshape(wide), step_down)
    with jax.named_scope("early_partner"):
        slot_major = jnp.stack(
            [
                left_statistic.astype(jnp.bfloat16),
                right_statistic.astype(jnp.bfloat16),
                left_basis,
                right_basis,
            ],
            axis=1,
        )
        outgoing, _ = tie((pick(slot_major, 1 - slot), from_partner))
        got = send(outgoing, partner)
        got, from_down, from_up = tie((got, from_down, from_up))
        early = jnp.concatenate(ordered(slot, pick(slot_major, slot), got), axis=-2)
        left_rows = early[2]
    with jax.named_scope("sum_groups_rest"):
        halfway = from_partner.astype(jnp.float32) + pick(opposite, slot).astype(jnp.float32)
        from_across = send(halfway.astype(jnp.bfloat16), step_across)
        near = (
            from_down.astype(jnp.float32)
            + from_up.astype(jnp.float32)
            + chunk(0).reshape(wide).astype(jnp.float32)
        ).reshape(2, piece_rows, 4 * size)
        to_next = pick(near, 1 - slot).astype(jnp.bfloat16)
        from_next = send(to_next, partner)
        summed = (
            pick(near, slot) + from_next.astype(jnp.float32) + from_across.astype(jnp.float32)
        ).astype(jnp.bfloat16)

    lefts, rights = early[0::2], early[1::2]
    same = jnp.where(side == 0, lefts, rights)
    cross = jnp.where(side == 0, rights, lefts)

    with jax.named_scope("spread"):
        tiles = summed.reshape(4, 16, 4, 8, 128).transpose(0, 3, 2, 1, 4).reshape(lanes, 64, 128)
        spread = lax.all_to_all(tiles, "tensor", 0, 0, tiled=True)
    with jax.named_scope("early_near"):
        cross, _ = tie((cross, to_next))
        near_up, near_down = send(cross, step_up), send(cross, step_down)
        across = send(same, step_across)
    with jax.named_scope("dispatch"):
        band, column = position_block // 4, position_block % 4
        entry = band[:, None] * 8 + jnp.arange(2, dtype=jnp.int32)[None, :] * 4 + column[:, None]
        routed = (
            spread.reshape(128, 16, 128)
            .at[entry.reshape(128)]
            .get(mode="promise_in_bounds")
            .reshape(lanes, 64, 128)
        )
        near_up, near_down, routed = tie((near_up, near_down, routed))
        arrived = lax.all_to_all(routed, "tensor", 0, 0, tiled=True)
    with jax.named_scope("gather_grad"):
        across, arrived = tie((across, arrived))
        by_slot = arrived.reshape(lanes, 2, 32, 128)

        def natural(tiles):
            return (
                tiles.reshape(4, 8, 2, 16, 128)
                .transpose(2, 0, 3, 1, 4)
                .reshape(2, piece_rows, size)
            )

        grad_wire = lax.dynamic_index_in_dim(by_slot, 1 - slot, 1, keepdims=False)
        grad_mine = natural(lax.dynamic_index_in_dim(by_slot, slot, 1, keepdims=False))
        grad_wire, grad_mine = tie((grad_wire, grad_mine))
        got_grad = send(grad_wire, partner)
        mine_pieces = around(grad_mine)
        got_grad, mine_pieces = tie((got_grad, mine_pieces))
        got_pieces = around(natural(got_grad))
    with jax.named_scope("early_product"):
        across, _ = tie((across, got_grad))
        early_power, item = statistic_times_basis(info, (same, near_up, across, near_down))
    with jax.named_scope("late_gather"):
        moments = jnp.stack([first_moment, second_moment], axis=1)
        moment_wire = pick(moments, 1 - slot)
        same_late, cross_late, moment_wire, got_pieces = tie(
            (same[1], cross[1], moment_wire, got_pieces)
        )
        other_pieces = (
            cross_late,
            send(same_late, step_up),
            send(cross_late, step_across),
            send(same_late, step_down),
        )
        got_moments = send(moment_wire, partner)
    with jax.named_scope("frame_first"):
        grad, framed_low, gram_rest, tall_rest = frame_first(
            info, mine_pieces + got_pieces, item, early_power
        )
    with jax.named_scope("rotate"):
        other_pieces, got_moments, grad = tie((other_pieces, got_moments, grad))
        moment_rows = jnp.concatenate(
            ordered(slot, pick(moments, slot), got_moments), axis=-2
        )
        returned, keep16, keep32, wire = rotate(
            info, grad, item, other_pieces, moment_rows[0], moment_rows[1]
        )
    with jax.named_scope("exchange"):
        returned_full = lax.all_gather(
            returned,
            "dp",
            axis=1,
            tiled=True,
            axis_index_groups=[[0, 2, 4, 6], [1, 3, 5, 7]],
        ).reshape(size, size)
        got = send(wire, partner)
    with jax.named_scope("frame_second"):
        gram_rest, _ = tie((gram_rest, returned))
        framed_high = frame_second(gram_rest, tall_rest)
        framed = jnp.concatenate([framed_low, framed_high], axis=1)
        left_rows, framed = tie((left_rows, framed))
        back = lax.all_to_all(
            framed.reshape(8, piece_rows, size), "dp", 0, 0, tiled=True
        ).reshape(2, 2, 2, piece_rows, size)
    with jax.named_scope("update"):
        mine, theirs = update_rows(info, left_rows, returned_full)
        update = jnp.stack(ordered(slot, mine, send(theirs, partner)))
        moment_next = jnp.stack(ordered(slot, keep16[0], got[0]))
        second_next = jnp.stack(ordered(slot, keep16[1], got[1]))

        def statistic_next(statistic, kept, came):
            outer = jnp.stack(ordered(slot, kept, came.astype(jnp.float32)))
            return BETA_STATS * statistic + (1.0 - BETA_STATS) * outer

        left_next = statistic_next(left_statistic, keep32[0], got[2])
        right_next = statistic_next(right_statistic, keep32[1], got[3])
    with jax.named_scope("renew"):
        marker = listed[:, None, None, None]
        renewed = back.transpose(1, 2, 0, 3, 4)
        left_basis_next = jnp.where(marker, renewed[0], left_basis)
        right_basis_next = jnp.where(marker, renewed[1], right_basis)
    return (
        update,
        moment_next,
        second_next,
        left_next,
        right_next,
        left_basis_next,
        right_basis_next,
    )


def solution(mesh):
    held = P("tensor", None, "dp", None)
    in_specs = (P("dp", "tensor", None), P(), P()) + (held,) * 6
    out_specs = (held,) * 7
    return jax.shard_map(body, mesh=mesh, in_specs=in_specs, out_specs=out_specs, check_vma=False)
```

```python
import functools
import jax
import jax.numpy as jnp
from jax import lax
from jax.experimental import pallas as pl
from jax.experimental.pallas import tpu as pltpu
from jax.sharding import PartitionSpec as P

BETA_MOMENT = 0.9
BETA_SQUARE = 0.95
BETA_STATS = 0.95
EPSILON = 1e-08
NT = (((1,), (1,)), ((), ()))
NN = (((1,), (0,)), ((), ()))
TN = (((0,), (0,)), ((), ()))


def split(x):
    high = x.astype(jnp.bfloat16)
    low = (x - high.astype(jnp.float32)).astype(jnp.bfloat16)
    return high, low


def dot(a, b, dims):
    return lax.dot_general(a, b, dims, preferred_element_type=jnp.float32)


def dot3(a, b, dims):
    (ah, al), (bh, bl) = a, b
    return dot(ah, bh, dims) + (dot(ah, bl, dims) + dot(al, bh, dims))


def inverse_factor(square, work, side, band=32):
    work[...] = square
    row8 = lax.broadcasted_iota(jnp.int32, (8, side), 0)
    lane8 = lax.broadcasted_iota(jnp.int32, (8, side), 1)
    groups = band // 8
    for start in range(0, side, band):
        rows = [work[start + 8 * q : start + 8 * q + 8, :] for q in range(groups)]
        pivots = []
        for q in range(groups):
            first = start + 8 * q
            cols = [
                [jnp.broadcast_to(rows[r][:, first + j : first + j + 1], (8, side)) for r in range(q, groups)]
                for j in range(8)
            ]
            kept = jnp.ones((8, side), jnp.float32)
            for j in range(8):
                pivot = jnp.broadcast_to(cols[j][0][j : j + 1, :], (8, side))
                kept = jnp.where(row8 == j, pivot, kept)
                inverse = 1.0 / pivot
                scaled = [c * inverse for c in cols[j]]
                scaled[0] = jnp.where(row8 > j, scaled[0], 0.0)
                for k in range(j + 1, 8):
                    lead = jnp.broadcast_to(cols[k][0][j : j + 1, :], (8, side))
                    cols[k] = [c - m * lead for c, m in zip(cols[k], scaled)]
                lead = jnp.broadcast_to(rows[q][j : j + 1, :], (8, side))
                for r in range(q, groups):
                    m = scaled[r - q]
                    mask = lane8 == first + j
                    if r == q:
                        mask = mask & (row8 > j)
                    rows[r] = jnp.where(mask, -m, rows[r] - m * lead)
            pivots.append(kept)
        done = []
        for q in range(groups):
            r = rows[q]
            first = start + 8 * q
            diag = row8 + first
            r = jnp.where(lane8 == diag, 1.0, r) * lax.rsqrt(pivots[q])
            done.append(r)
        panel = jnp.concatenate(done, axis=0)
        rowb = lax.broadcasted_iota(jnp.int32, (band, side), 0) + start
        laneb = lax.broadcasted_iota(jnp.int32, (band, side), 1)
        lower = jnp.where(laneb > rowb, jnp.where(laneb < start + band, 0.0, panel), panel)
        stop = start + band
        if stop < side:
            work[start:stop, :] = jnp.where(laneb > rowb, 0.0, panel)
            rest = side - stop
            upper = jnp.transpose(panel)[stop:, :]
            change = dot3(split(upper), split(lower), NN)
            lane = lax.broadcasted_iota(jnp.int32, (rest, side), 1)
            old = work[stop:, :]
            work[stop:, :] = jnp.where((lane >= start) & (lane < stop), 0.0, old) - change
        else:
            work[start:stop, :] = jnp.where(laneb > rowb, 0.0, panel)
    return work[...]


def vmem(count):
    return [pl.BlockSpec(memory_space=pltpu.VMEM)] * count


SMEM = pl.BlockSpec(memory_space=pltpu.SMEM)
PARAMS = pltpu.CompilerParams(vmem_limit_bytes=48 * 1024 * 1024)


def cost(flops, size):
    return pl.CostEstimate(flops=flops, bytes_accessed=size, transcendentals=0)


def place(pieces, ring, whole, first=0, count=128):
    for piece, shift in zip(pieces, (0, 3, 2, 1)):
        at = lax.rem(ring + shift, 4) * 128 + first
        for h in range(2):
            whole[pl.ds(pl.multiple_of(h * 512 + at, 64), count), :] = piece[h][...]


def statistic_kernel(info, a0, a1, a2, a3, out_ref, basis_ref, stat):
    ring = info[0]
    pieces = (a0, a1, a2, a3)
    place([p.at[0] for p in pieces], ring, stat)
    place([p.at[1] for p in pieces], ring, basis_ref)
    basis = basis_ref[...]
    for r in range(0, 1024, 256):
        out_ref[r : r + 256, :] = dot(stat[r : r + 256, :], basis, NN)


def statistic_times_basis(info, pieces):
    return pl.pallas_call(
        statistic_kernel,
        out_shape=(
            jax.ShapeDtypeStruct((1024, 1024), jnp.float32),
            jax.ShapeDtypeStruct((1024, 1024), jnp.bfloat16),
        ),
        in_specs=[SMEM] + vmem(4),
        out_specs=tuple(vmem(2)),
        scratch_shapes=[pltpu.VMEM((1024, 1024), jnp.bfloat16)],
        compiler_params=PARAMS,
        cost_estimate=cost(2 * 1024**3, 10 * 2**20),
    )(info, *pieces)


def rotate_kernel(
    info, grad, item, o0, o1, o2, o3, first, second,
    returned, keep16, keep32, wire, other, lhs, step,
):
    ring, slot, side = info[0], info[1], info[2]
    place((o0, o1, o2, o3), ring, other)
    whole = grad[...]

    def divide(rows, h, keep, index, place_on_wire):
        low, high = rows[:64], rows[64:]
        keep[index, h] = jnp.where(slot == 0, low, high).astype(keep.dtype)
        wire[place_on_wire, h] = jnp.where(slot == 0, high, low).astype(wire.dtype)

    def run(left, right):
        for h in range(2):
            at = pl.multiple_of(h * 512 + ring * 128, 128)
            lhs[h * 128 : h * 128 + 128, :] = dot(left[:, pl.ds(at, 128)], whole, TN).astype(
                jnp.bfloat16
            )
        step[...] = dot(lhs[...], right[...], NN)
        for h in range(2):
            rotated = step[h * 128 : h * 128 + 128, :]
            moment = BETA_MOMENT * first[h].astype(jnp.float32) + (1.0 - BETA_MOMENT) * rotated
            square = (
                BETA_SQUARE * second[h].astype(jnp.float32)
                + (1.0 - BETA_SQUARE) * rotated * rotated
            )
            divide(moment, h, keep16, 0, 0)
            divide(square, h, keep16, 1, 1)
            lhs[h * 128 : h * 128 + 128, :] = (moment / (jnp.sqrt(square) + EPSILON)).astype(
                jnp.bfloat16
            )
        back = dot(lhs[...], right[...], NT)
        for h in range(2):
            returned[h] = back[h * 128 : h * 128 + 128].astype(jnp.bfloat16)

    @pl.when(side == 0)
    def _():
        run(item, other)

    @pl.when(side == 1)
    def _():
        run(other, item)

    for h in range(2):
        at = pl.multiple_of(h * 512 + ring * 128, 128)
        divide(dot(grad[pl.ds(at, 128), :], whole, NT), h, keep32, 0, 2)
        divide(dot(grad[:, pl.ds(at, 128)], whole, TN), h, keep32, 1, 3)


def rotate(info, grad, item, other_pieces, first, second):
    shape = jax.ShapeDtypeStruct
    return pl.pallas_call(
        rotate_kernel,
        out_shape=(
            shape((2, 128, 1024), jnp.bfloat16),
            shape((2, 2, 64, 1024), jnp.bfloat16),
            shape((2, 2, 64, 1024), jnp.float32),
            shape((4, 2, 64, 1024), jnp.bfloat16),
        ),
        in_specs=[SMEM] + vmem(8),
        out_specs=tuple(vmem(4)),
        scratch_shapes=[
            pltpu.VMEM((1024, 1024), jnp.bfloat16),
            pltpu.VMEM((256, 1024), jnp.bfloat16),
            pltpu.VMEM((256, 1024), jnp.float32),
        ],
        compiler_params=PARAMS,
        cost_estimate=cost(5 * 512 * 1024**2, 13 * 2**20),
    )(info, grad, item, *other_pieces, first, second)


def update_kernel(info, rows, r0, r1, r2, r3, keep, wire, whole):
    ring, slot = info[0], info[1]
    place((r0, r1, r2, r3), ring, whole)
    for h in range(2):
        out = dot(rows[h], whole[...], NN)
        low, high = out[:64], out[64:]
        keep[h] = jnp.where(slot == 0, low, high).astype(keep.dtype)
        wire[h] = jnp.where(slot == 0, high, low).astype(wire.dtype)


def update_rows(info, rows, pieces):
    shape = jax.ShapeDtypeStruct((2, 64, 1024), jnp.bfloat16)
    return pl.pallas_call(
        update_kernel,
        out_shape=(shape, shape),
        in_specs=[SMEM] + vmem(5),
        out_specs=tuple(vmem(2)),
        scratch_shapes=[pltpu.VMEM((1024, 1024), jnp.bfloat16)],
        compiler_params=PARAMS,
        cost_estimate=cost(512 * 1024**2, 4 * 2**20),
    )(info, rows, *pieces)


def eliminate(gram, tall, work, out_ref, stop, side):
    size = gram.shape[0]
    for k in range(0, stop, side):
        e = k + side
        inv = inverse_factor(gram[k:e, k:e], work, side)
        invs = split(inv)
        own = dot3(split(tall[:, k:e]), invs, NT)
        out_ref[:, k:e] = own.astype(out_ref.dtype)
        if e < size:
            below = dot3(split(gram[e:, k:e]), invs, NT)
            bh, bl = split(below)
            oh, ol = split(own)
            for c in range(e, size, side):
                lo = c - e
                pair = (bh[lo : lo + side], bl[lo : lo + side])
                gram[c:, c : c + side] = gram[c:, c : c + side] - dot3((bh[lo:], bl[lo:]), pair, NT)
                tall[:, c : c + side] = tall[:, c : c + side] - dot3((oh, ol), pair, NT)


def frame_first_kernel(
    info, m0, m1, m2, m3, t0, t1, t2, t3, basis, early,
    grad, out_ref, gram_rest, tall_rest, gram, tall, work, outer, power, *, side,
):
    size, part = gram.shape[0], tall.shape[0]
    stop = out_ref.shape[1]
    ring, slot = info[0], info[1]
    place((m0, m1, m2, m3), ring, grad, slot * 64, 64)
    place((t0, t1, t2, t3), ring, grad, (1 - slot) * 64, 64)

    @pl.when(info[2] == 0)
    def _():
        for c in range(0, size, 256):
            outer[c : c + 256, :] = dot(grad[c : c + 256, :], grad[...], NT).astype(jnp.bfloat16)

    @pl.when(info[2] == 1)
    def _():
        for c in range(0, size, 256):
            outer[c : c + 256, :] = dot(grad[:, c : c + 256], grad[...], TN).astype(jnp.bfloat16)

    for c in range(0, size, 256):
        power[c : c + 256, :] = (
            BETA_STATS * early[c : c + 256, :]
            + (1.0 - BETA_STATS) * dot(outer[c : c + 256, :], basis[...], NN)
        ).astype(jnp.bfloat16)
    for c in range(0, size, 256):
        gram[c:, c : c + 256] = dot(power[:, c:], power[:, c : c + 256], TN)
    tall[...] = power[pl.ds(pl.multiple_of(info[3] * part, part), part), :].astype(jnp.float32)
    eliminate(gram, tall, work, out_ref, stop, side)
    gram_rest[...] = gram[stop:, stop:]
    tall_rest[...] = tall[:, stop:]


def frame_first(info, grad_pieces, basis, early, stop=512, side=128):
    size = basis.shape[0]
    part = size // 2
    shape = jax.ShapeDtypeStruct
    return pl.pallas_call(
        functools.partial(frame_first_kernel, side=side),
        out_shape=(
            shape((size, size), jnp.bfloat16),
            shape((part, stop), jnp.bfloat16),
            shape((size - stop, size - stop), jnp.float32),
            shape((part, size - stop), jnp.float32),
        ),
        in_specs=[SMEM] + vmem(10),
        out_specs=tuple(vmem(4)),
        scratch_shapes=[
            pltpu.VMEM((size, size), jnp.float32),
            pltpu.VMEM((part, size), jnp.float32),
            pltpu.VMEM((side, side), jnp.float32),
            pltpu.VMEM((size, size), jnp.bfloat16),
            pltpu.VMEM((size, size), jnp.bfloat16),
        ],
        compiler_params=PARAMS,
        cost_estimate=cost(30 * 10**9, 12 * 2**20),
    )(info, *grad_pieces, basis, early)


def frame_second_kernel(gram_rest, tall_rest, out_ref, gram, tall, work, *, side):
    gram[...] = gram_rest[...]
    tall[...] = tall_rest[...]
    eliminate(gram, tall, work, out_ref, gram.shape[0], side)


def frame_second(gram_rest, tall_rest, side=128):
    return pl.pallas_call(
        functools.partial(frame_second_kernel, side=side),
        out_shape=jax.ShapeDtypeStruct(tall_rest.shape, jnp.bfloat16),
        in_specs=vmem(2),
        out_specs=pl.BlockSpec(memory_space=pltpu.VMEM),
        scratch_shapes=[
            pltpu.VMEM(gram_rest.shape, jnp.float32),
            pltpu.VMEM(tall_rest.shape, jnp.float32),
            pltpu.VMEM((side, side), jnp.float32),
        ],
        compiler_params=PARAMS,
        cost_estimate=cost(20 * 10**9, 3 * 2**20),
    )(gram_rest, tall_rest)


def step_up(i):
    return ((i // 2 + 1) % 4) * 2 + i % 2


def step_down(i):
    return ((i // 2 + 3) % 4) * 2 + i % 2


def step_across(i):
    return ((i // 2 + 2) % 4) * 2 + i % 2


def partner(i):
    return i ^ 1


def send(values, route):
    return lax.ppermute(values, "dp", [(i, route(i)) for i in range(8)])


def ordered(flag, mine, theirs):
    return jnp.where(flag == 0, mine, theirs), jnp.where(flag == 0, theirs, mine)


def pick(stacked, index):
    return lax.dynamic_index_in_dim(stacked, index, 0, keepdims=False)


tie = lax.optimization_barrier


def body(
    gradient_parts,
    block_owner,
    refresh_list,
    first_moment,
    second_moment,
    left_statistic,
    right_statistic,
    left_basis,
    right_basis,
):
    own_group = lax.axis_index("dp")
    own_lane = lax.axis_index("tensor")
    ring, slot = own_group // 2, own_group % 2
    side, half = ring % 2, ring // 2
    info = jnp.stack([ring, slot, side, half]).astype(jnp.int32)
    piece = first_moment.shape
    slot_count, _, piece_rows, size = piece
    lanes = 32

    def around(pair):
        return pair, send(pair, step_up), send(pair, step_across), send(pair, step_down)

    position_block = jnp.argsort(block_owner)
    owned_blocks = lax.dynamic_slice_in_dim(position_block, own_lane * slot_count, slot_count)
    listed = jnp.any(refresh_list[None, :] == owned_blocks[:, None], axis=1)

    with jax.named_scope("sum_groups"):
        chunks = gradient_parts.reshape(4, 2, piece_rows, 4 * size)

        def chunk(shift):
            return pick(chunks, (ring + shift) % 4)

        wide = (2 * piece_rows, 4 * size)
        opposite = chunk(2)
        from_partner = send(pick(opposite, 1 - slot), partner)
        from_down = send(chunk(1).reshape(wide), step_up)
        from_up = send(chunk(3).reshape(wide), step_down)
    with jax.named_scope("early_partner"):
        slot_major = jnp.stack(
            [
                left_statistic.astype(jnp.bfloat16),
                right_statistic.astype(jnp.bfloat16),
                left_basis,
                right_basis,
            ],
            axis=1,
        )
        outgoing, _ = tie((pick(slot_major, 1 - slot), from_partner))
        got = send(outgoing, partner)
        got, from_down, from_up = tie((got, from_down, from_up))
        early = jnp.concatenate(ordered(slot, pick(slot_major, slot), got), axis=-2)
        left_rows = early[2]
    with jax.named_scope("sum_groups_rest"):
        halfway = from_partner.astype(jnp.float32) + pick(opposite, slot).astype(jnp.float32)
        from_across = send(halfway.astype(jnp.bfloat16), step_across)
        near = (
            from_down.astype(jnp.float32)
            + from_up.astype(jnp.float32)
            + chunk(0).reshape(wide).astype(jnp.float32)
        ).reshape(2, piece_rows, 4 * size)
        to_next = pick(near, 1 - slot).astype(jnp.bfloat16)
        from_next = send(to_next, partner)
        summed = (
            pick(near, slot) + from_next.astype(jnp.float32) + from_across.astype(jnp.float32)
        ).astype(jnp.bfloat16)

    lefts, rights = early[0::2], early[1::2]
    same = jnp.where(side == 0, lefts, rights)
    cross = jnp.where(side == 0, rights, lefts)

    with jax.named_scope("spread"):
        tiles = summed.reshape(4, 16, 4, 8, 128).transpose(0, 3, 2, 1, 4).reshape(lanes, 64, 128)
        spread = lax.all_to_all(tiles, "tensor", 0, 0, tiled=True)
    with jax.named_scope("early_near"):
        cross, _ = tie((cross, to_next))
        near_up, near_down = send(cross, step_up), send(cross, step_down)
        across = send(same, step_across)
    with jax.named_scope("dispatch"):
        band, column = position_block // 4, position_block % 4
        entry = band[:, None] * 8 + jnp.arange(2, dtype=jnp.int32)[None, :] * 4 + column[:, None]
        routed = (
            spread.reshape(128, 16, 128)
            .at[entry.reshape(128)]
            .get(mode="promise_in_bounds")
            .reshape(lanes, 64, 128)
        )
        near_up, near_down, routed = tie((near_up, near_down, routed))
        arrived = lax.all_to_all(routed, "tensor", 0, 0, tiled=True)
    with jax.named_scope("gather_grad"):
        across, arrived = tie((across, arrived))
        by_slot = arrived.reshape(lanes, 2, 32, 128)

        def natural(tiles):
            return (
                tiles.reshape(4, 8, 2, 16, 128)
                .transpose(2, 0, 3, 1, 4)
                .reshape(2, piece_rows, size)
            )

        grad_wire = lax.dynamic_index_in_dim(by_slot, 1 - slot, 1, keepdims=False)
        grad_mine = natural(lax.dynamic_index_in_dim(by_slot, slot, 1, keepdims=False))
        grad_wire, grad_mine = tie((grad_wire, grad_mine))
        got_grad = send(grad_wire, partner)
        mine_pieces = around(grad_mine)
        got_grad, mine_pieces = tie((got_grad, mine_pieces))
        got_pieces = around(natural(got_grad))
    with jax.named_scope("early_product"):
        across, _ = tie((across, got_grad))
        early_power, item = statistic_times_basis(info, (same, near_up, across, near_down))
    with jax.named_scope("late_gather"):
        moments = jnp.stack([first_moment, second_moment], axis=1)
        moment_wire = pick(moments, 1 - slot)
        same_late, cross_late, moment_wire, got_pieces = tie(
            (same[1], cross[1], moment_wire, got_pieces)
        )
        other_pieces = (
            cross_late,
            send(same_late, step_up),
            send(cross_late, step_across),
            send(same_late, step_down),
        )
        got_moments = send(moment_wire, partner)
    with jax.named_scope("frame_first"):
        grad, framed_low, gram_rest, tall_rest = frame_first(
            info, mine_pieces + got_pieces, item, early_power
        )
    with jax.named_scope("rotate"):
        other_pieces, got_moments, grad = tie((other_pieces, got_moments, grad))
        moment_rows = jnp.concatenate(
            ordered(slot, pick(moments, slot), got_moments), axis=-2
        )
        returned, keep16, keep32, wire = rotate(
            info, grad, item, other_pieces, moment_rows[0], moment_rows[1]
        )
    with jax.named_scope("exchange"):
        up, down = send(returned, step_up), send(returned, step_down)
        returned_pieces = (returned, up, send(returned, step_across), down)
        got = send(wire, partner)
    with jax.named_scope("frame_second"):
        gram_rest, _ = tie((gram_rest, returned))
        framed_high = frame_second(gram_rest, tall_rest)
        framed = jnp.concatenate([framed_low, framed_high], axis=1)
        left_rows, framed = tie((left_rows, framed))
        back = lax.all_to_all(
            framed.reshape(8, piece_rows, size), "dp", 0, 0, tiled=True
        ).reshape(2, 2, 2, piece_rows, size)
    with jax.named_scope("update"):
        mine, theirs = update_rows(info, left_rows, returned_pieces)
        update = jnp.stack(ordered(slot, mine, send(theirs, partner)))
        moment_next = jnp.stack(ordered(slot, keep16[0], got[0]))
        second_next = jnp.stack(ordered(slot, keep16[1], got[1]))

        def statistic_next(statistic, kept, came):
            outer = jnp.stack(ordered(slot, kept, came.astype(jnp.float32)))
            return BETA_STATS * statistic + (1.0 - BETA_STATS) * outer

        left_next = statistic_next(left_statistic, keep32[0], got[2])
        right_next = statistic_next(right_statistic, keep32[1], got[3])
    with jax.named_scope("renew"):
        marker = listed[:, None, None, None]
        renewed = back.transpose(1, 2, 0, 3, 4)
        left_basis_next = jnp.where(marker, renewed[0], left_basis)
        right_basis_next = jnp.where(marker, renewed[1], right_basis)
    return (
        update,
        moment_next,
        second_next,
        left_next,
        right_next,
        left_basis_next,
        right_basis_next,
    )


def solution(mesh):
    held = P("tensor", None, "dp", None)
    in_specs = (P("dp", "tensor", None), P(), P()) + (held,) * 6
    out_specs = (held,) * 7
    return jax.shard_map(body, mesh=mesh, in_specs=in_specs, out_specs=out_specs, check_vma=False)
```

```python
import functools
import jax
import jax.numpy as jnp
from jax import lax
from jax.experimental import pallas as pl
from jax.experimental.pallas import tpu as pltpu
from jax.sharding import PartitionSpec as P

BETA_MOMENT = 0.9
BETA_SQUARE = 0.95
BETA_STATS = 0.95
EPSILON = 1e-08
NT = (((1,), (1,)), ((), ()))
NN = (((1,), (0,)), ((), ()))
TN = (((0,), (0,)), ((), ()))


def split(x):
    high = x.astype(jnp.bfloat16)
    low = (x - high.astype(jnp.float32)).astype(jnp.bfloat16)
    return high, low


def dot(a, b, dims):
    return lax.dot_general(a, b, dims, preferred_element_type=jnp.float32)


def dot3(a, b, dims):
    (ah, al), (bh, bl) = a, b
    return dot(ah, bh, dims) + (dot(ah, bl, dims) + dot(al, bh, dims))


def inverse_factor(square, work, side, band=32):
    work[...] = square
    row8 = lax.broadcasted_iota(jnp.int32, (8, side), 0)
    lane8 = lax.broadcasted_iota(jnp.int32, (8, side), 1)
    groups = band // 8
    for start in range(0, side, band):
        rows = [work[start + 8 * q : start + 8 * q + 8, :] for q in range(groups)]
        pivots = []
        for q in range(groups):
            first = start + 8 * q
            cols = [
                [jnp.broadcast_to(rows[r][:, first + j : first + j + 1], (8, side)) for r in range(q, groups)]
                for j in range(8)
            ]
            kept = jnp.ones((8, side), jnp.float32)
            for j in range(8):
                pivot = jnp.broadcast_to(cols[j][0][j : j + 1, :], (8, side))
                kept = jnp.where(row8 == j, pivot, kept)
                inverse = 1.0 / pivot
                scaled = [c * inverse for c in cols[j]]
                scaled[0] = jnp.where(row8 > j, scaled[0], 0.0)
                for k in range(j + 1, 8):
                    lead = jnp.broadcast_to(cols[k][0][j : j + 1, :], (8, side))
                    cols[k] = [c - m * lead for c, m in zip(cols[k], scaled)]
                lead = jnp.broadcast_to(rows[q][j : j + 1, :], (8, side))
                for r in range(q, groups):
                    m = scaled[r - q]
                    mask = lane8 == first + j
                    if r == q:
                        mask = mask & (row8 > j)
                    rows[r] = jnp.where(mask, -m, rows[r] - m * lead)
            pivots.append(kept)
        done = []
        for q in range(groups):
            r = rows[q]
            first = start + 8 * q
            diag = row8 + first
            r = jnp.where(lane8 == diag, 1.0, r) * lax.rsqrt(pivots[q])
            done.append(r)
        panel = jnp.concatenate(done, axis=0)
        rowb = lax.broadcasted_iota(jnp.int32, (band, side), 0) + start
        laneb = lax.broadcasted_iota(jnp.int32, (band, side), 1)
        lower = jnp.where(laneb > rowb, jnp.where(laneb < start + band, 0.0, panel), panel)
        stop = start + band
        if stop < side:
            work[start:stop, :] = jnp.where(laneb > rowb, 0.0, panel)
            rest = side - stop
            upper = jnp.transpose(panel)[stop:, :]
            change = dot3(split(upper), split(lower), NN)
            lane = lax.broadcasted_iota(jnp.int32, (rest, side), 1)
            old = work[stop:, :]
            work[stop:, :] = jnp.where((lane >= start) & (lane < stop), 0.0, old) - change
        else:
            work[start:stop, :] = jnp.where(laneb > rowb, 0.0, panel)
    return work[...]


def vmem(count):
    return [pl.BlockSpec(memory_space=pltpu.VMEM)] * count


SMEM = pl.BlockSpec(memory_space=pltpu.SMEM)
PARAMS = pltpu.CompilerParams(vmem_limit_bytes=48 * 1024 * 1024)


def cost(flops, size):
    return pl.CostEstimate(flops=flops, bytes_accessed=size, transcendentals=0)


def place(pieces, ring, whole, first=0, count=128):
    for piece, shift in zip(pieces, (0, 3, 2, 1)):
        at = lax.rem(ring + shift, 4) * 128 + first
        for h in range(2):
            whole[pl.ds(pl.multiple_of(h * 512 + at, 64), count), :] = piece[h][...]


def statistic_kernel(info, a0, a1, a2, a3, out_ref, basis_ref, stat):
    ring = info[0]
    pieces = (a0, a1, a2, a3)
    place([p.at[0] for p in pieces], ring, stat)
    place([p.at[1] for p in pieces], ring, basis_ref)
    basis = basis_ref[...]
    for r in range(0, 1024, 256):
        out_ref[r : r + 256, :] = dot(stat[r : r + 256, :], basis, NN)


def statistic_times_basis(info, pieces):
    return pl.pallas_call(
        statistic_kernel,
        out_shape=(
            jax.ShapeDtypeStruct((1024, 1024), jnp.float32),
            jax.ShapeDtypeStruct((1024, 1024), jnp.bfloat16),
        ),
        in_specs=[SMEM] + vmem(4),
        out_specs=tuple(vmem(2)),
        scratch_shapes=[pltpu.VMEM((1024, 1024), jnp.bfloat16)],
        compiler_params=PARAMS,
        cost_estimate=cost(2 * 1024**3, 10 * 2**20),
    )(info, *pieces)


def rotate_kernel(
    info, grad, item, o0, o1, o2, o3, first, second,
    returned, keep16, keep32, wire, other, lhs, step,
):
    ring, slot, side = info[0], info[1], info[2]
    place((o0, o1, o2, o3), ring, other)
    whole = grad[...]

    def divide(rows, h, keep, index, place_on_wire):
        low, high = rows[:64], rows[64:]
        keep[index, h] = jnp.where(slot == 0, low, high).astype(keep.dtype)
        wire[place_on_wire, h] = jnp.where(slot == 0, high, low).astype(wire.dtype)

    def run(left, right):
        for h in range(2):
            at = pl.multiple_of(h * 512 + ring * 128, 128)
            lhs[h * 128 : h * 128 + 128, :] = dot(left[:, pl.ds(at, 128)], whole, TN).astype(
                jnp.bfloat16
            )
        step[...] = dot(lhs[...], right[...], NN)
        for h in range(2):
            rotated = step[h * 128 : h * 128 + 128, :]
            moment = BETA_MOMENT * first[h].astype(jnp.float32) + (1.0 - BETA_MOMENT) * rotated
            square = (
                BETA_SQUARE * second[h].astype(jnp.float32)
                + (1.0 - BETA_SQUARE) * rotated * rotated
            )
            divide(moment, h, keep16, 0, 0)
            divide(square, h, keep16, 1, 1)
            lhs[h * 128 : h * 128 + 128, :] = (moment / (jnp.sqrt(square) + EPSILON)).astype(
                jnp.bfloat16
            )
        back = dot(lhs[...], right[...], NT)
        for h in range(2):
            returned[h] = back[h * 128 : h * 128 + 128].astype(jnp.bfloat16)

    @pl.when(side == 0)
    def _():
        run(item, other)

    @pl.when(side == 1)
    def _():
        run(other, item)

    for h in range(2):
        at = pl.multiple_of(h * 512 + ring * 128, 128)
        divide(dot(grad[pl.ds(at, 128), :], whole, NT), h, keep32, 0, 2)
        divide(dot(grad[:, pl.ds(at, 128)], whole, TN), h, keep32, 1, 3)


def rotate(info, grad, item, other_pieces, first, second):
    shape = jax.ShapeDtypeStruct
    return pl.pallas_call(
        rotate_kernel,
        out_shape=(
            shape((2, 128, 1024), jnp.bfloat16),
            shape((2, 2, 64, 1024), jnp.bfloat16),
            shape((2, 2, 64, 1024), jnp.float32),
            shape((4, 2, 64, 1024), jnp.bfloat16),
        ),
        in_specs=[SMEM] + vmem(8),
        out_specs=tuple(vmem(4)),
        scratch_shapes=[
            pltpu.VMEM((1024, 1024), jnp.bfloat16),
            pltpu.VMEM((256, 1024), jnp.bfloat16),
            pltpu.VMEM((256, 1024), jnp.float32),
        ],
        compiler_params=PARAMS,
        cost_estimate=cost(5 * 512 * 1024**2, 13 * 2**20),
    )(info, grad, item, *other_pieces, first, second)


def update_kernel(info, rows, r0, r1, r2, r3, keep, wire, whole):
    ring, slot = info[0], info[1]
    place((r0, r1, r2, r3), ring, whole)
    for h in range(2):
        out = dot(rows[h], whole[...], NN)
        low, high = out[:64], out[64:]
        keep[h] = jnp.where(slot == 0, low, high).astype(keep.dtype)
        wire[h] = jnp.where(slot == 0, high, low).astype(wire.dtype)


def update_rows(info, rows, pieces):
    shape = jax.ShapeDtypeStruct((2, 64, 1024), jnp.bfloat16)
    return pl.pallas_call(
        update_kernel,
        out_shape=(shape, shape),
        in_specs=[SMEM] + vmem(5),
        out_specs=tuple(vmem(2)),
        scratch_shapes=[pltpu.VMEM((1024, 1024), jnp.bfloat16)],
        compiler_params=PARAMS,
        cost_estimate=cost(512 * 1024**2, 4 * 2**20),
    )(info, rows, *pieces)


def eliminate(gram, tall, work, out_ref, stop, side):
    size = gram.shape[0]
    for k in range(0, stop, side):
        e = k + side
        inv = inverse_factor(gram[k:e, k:e], work, side)
        invs = split(inv)
        own = dot3(split(tall[:, k:e]), invs, NT)
        out_ref[:, k:e] = own.astype(out_ref.dtype)
        if e < size:
            below = dot3(split(gram[e:, k:e]), invs, NT)
            bh, bl = split(below)
            oh, ol = split(own)
            for c in range(e, size, side):
                lo = c - e
                pair = (bh[lo : lo + side], bl[lo : lo + side])
                gram[c:, c : c + side] = gram[c:, c : c + side] - dot3((bh[lo:], bl[lo:]), pair, NT)
                tall[:, c : c + side] = tall[:, c : c + side] - dot3((oh, ol), pair, NT)


def frame_first_kernel(
    info, m0, m1, m2, m3, t0, t1, t2, t3, basis, early,
    grad, out_ref, gram_rest, tall_rest, gram, tall, work, outer, power, *, side,
):
    size, part = gram.shape[0], tall.shape[0]
    stop = out_ref.shape[1]
    ring, slot = info[0], info[1]
    place((m0, m1, m2, m3), ring, grad, slot * 64, 64)
    place((t0, t1, t2, t3), ring, grad, (1 - slot) * 64, 64)

    @pl.when(info[2] == 0)
    def _():
        for c in range(0, size, 256):
            outer[c : c + 256, :] = dot(grad[c : c + 256, :], grad[...], NT).astype(jnp.bfloat16)

    @pl.when(info[2] == 1)
    def _():
        for c in range(0, size, 256):
            outer[c : c + 256, :] = dot(grad[:, c : c + 256], grad[...], TN).astype(jnp.bfloat16)

    for c in range(0, size, 256):
        power[c : c + 256, :] = (
            BETA_STATS * early[c : c + 256, :]
            + (1.0 - BETA_STATS) * dot(outer[c : c + 256, :], basis[...], NN)
        ).astype(jnp.bfloat16)
    for c in range(0, size, 256):
        gram[c:, c : c + 256] = dot(power[:, c:], power[:, c : c + 256], TN)
    tall[...] = power[pl.ds(pl.multiple_of(info[3] * part, part), part), :].astype(jnp.float32)
    eliminate(gram, tall, work, out_ref, stop, side)
    gram_rest[...] = gram[stop:, stop:]
    tall_rest[...] = tall[:, stop:]


def frame_first(info, grad_pieces, basis, early, stop=512, side=128):
    size = basis.shape[0]
    part = size // 2
    shape = jax.ShapeDtypeStruct
    return pl.pallas_call(
        functools.partial(frame_first_kernel, side=side),
        out_shape=(
            shape((size, size), jnp.bfloat16),
            shape((part, stop), jnp.bfloat16),
            shape((size - stop, size - stop), jnp.float32),
            shape((part, size - stop), jnp.float32),
        ),
        in_specs=[SMEM] + vmem(10),
        out_specs=tuple(vmem(4)),
        scratch_shapes=[
            pltpu.VMEM((size, size), jnp.float32),
            pltpu.VMEM((part, size), jnp.float32),
            pltpu.VMEM((side, side), jnp.float32),
            pltpu.VMEM((size, size), jnp.bfloat16),
            pltpu.VMEM((size, size), jnp.bfloat16),
        ],
        compiler_params=PARAMS,
        cost_estimate=cost(30 * 10**9, 12 * 2**20),
    )(info, *grad_pieces, basis, early)


def frame_second_kernel(gram_rest, tall_rest, out_ref, gram, tall, work, *, side):
    gram[...] = gram_rest[...]
    tall[...] = tall_rest[...]
    eliminate(gram, tall, work, out_ref, gram.shape[0], side)


def frame_second(gram_rest, tall_rest, side=128):
    return pl.pallas_call(
        functools.partial(frame_second_kernel, side=side),
        out_shape=jax.ShapeDtypeStruct(tall_rest.shape, jnp.bfloat16),
        in_specs=vmem(2),
        out_specs=pl.BlockSpec(memory_space=pltpu.VMEM),
        scratch_shapes=[
            pltpu.VMEM(gram_rest.shape, jnp.float32),
            pltpu.VMEM(tall_rest.shape, jnp.float32),
            pltpu.VMEM((side, side), jnp.float32),
        ],
        compiler_params=PARAMS,
        cost_estimate=cost(20 * 10**9, 3 * 2**20),
    )(gram_rest, tall_rest)


def step_up(i):
    return ((i // 2 + 1) % 4) * 2 + i % 2


def step_down(i):
    return ((i // 2 + 3) % 4) * 2 + i % 2


def step_across(i):
    return ((i // 2 + 2) % 4) * 2 + i % 2


def partner(i):
    return i ^ 1


def send(values, route):
    return lax.ppermute(values, "dp", [(i, route(i)) for i in range(8)])


def ordered(flag, mine, theirs):
    return jnp.where(flag == 0, mine, theirs), jnp.where(flag == 0, theirs, mine)


def pick(stacked, index):
    return lax.dynamic_index_in_dim(stacked, index, 0, keepdims=False)


tie = lax.optimization_barrier


def body(
    gradient_parts,
    block_owner,
    refresh_list,
    first_moment,
    second_moment,
    left_statistic,
    right_statistic,
    left_basis,
    right_basis,
):
    own_group = lax.axis_index("dp")
    own_lane = lax.axis_index("tensor")
    ring, slot = own_group // 2, own_group % 2
    side, half = ring % 2, ring // 2
    info = jnp.stack([ring, slot, side, half]).astype(jnp.int32)
    piece = first_moment.shape
    slot_count, _, piece_rows, size = piece
    lanes = 32

    def around(pair):
        return pair, send(pair, step_up), send(pair, step_across), send(pair, step_down)

    position_block = jnp.argsort(block_owner)
    owned_blocks = lax.dynamic_slice_in_dim(position_block, own_lane * slot_count, slot_count)
    listed = jnp.any(refresh_list[None, :] == owned_blocks[:, None], axis=1)

    with jax.named_scope("sum_groups"):
        chunks = gradient_parts.reshape(4, 2, piece_rows, 4 * size)

        def chunk(shift):
            return pick(chunks, (ring + shift) % 4)

        wide = (2 * piece_rows, 4 * size)
        opposite = chunk(2)
        from_partner = send(pick(opposite, 1 - slot), partner)
        from_down = send(chunk(1).reshape(wide), step_up)
        from_up = send(chunk(3).reshape(wide), step_down)
    with jax.named_scope("early_partner"):
        slot_major = jnp.stack(
            [
                left_statistic.astype(jnp.bfloat16),
                right_statistic.astype(jnp.bfloat16),
                left_basis,
                right_basis,
            ],
            axis=1,
        )
        outgoing, _ = tie((pick(slot_major, 1 - slot), from_partner))
        got = send(outgoing, partner)
        got, from_down, from_up = tie((got, from_down, from_up))
        early = jnp.concatenate(ordered(slot, pick(slot_major, slot), got), axis=-2)
        left_rows = early[2]
    with jax.named_scope("sum_groups_rest"):
        halfway = from_partner.astype(jnp.float32) + pick(opposite, slot).astype(jnp.float32)
        from_across = send(halfway.astype(jnp.bfloat16), step_across)
        near = (
            from_down.astype(jnp.float32)
            + from_up.astype(jnp.float32)
            + chunk(0).reshape(wide).astype(jnp.float32)
        ).reshape(2, piece_rows, 4 * size)
        to_next = pick(near, 1 - slot).astype(jnp.bfloat16)
        from_next = send(to_next, partner)
        summed = (
            pick(near, slot) + from_next.astype(jnp.float32) + from_across.astype(jnp.float32)
        ).astype(jnp.bfloat16)

    lefts, rights = early[0::2], early[1::2]
    same = jnp.where(side == 0, lefts, rights)
    cross = jnp.where(side == 0, rights, lefts)

    with jax.named_scope("spread"):
        tiles = summed.reshape(4, 16, 4, 8, 128).transpose(0, 3, 2, 1, 4).reshape(lanes, 64, 128)
        spread = lax.all_to_all(tiles, "tensor", 0, 0, tiled=True)
    with jax.named_scope("early_near"):
        cross, _ = tie((cross, to_next))
        near_up, near_down = send(cross, step_up), send(cross, step_down)
        across = send(same, step_across)
    with jax.named_scope("dispatch"):
        band, column = position_block // 4, position_block % 4
        entry = band[:, None] * 8 + jnp.arange(2, dtype=jnp.int32)[None, :] * 4 + column[:, None]
        routed = (
            spread.reshape(128, 16, 128)
            .at[entry.reshape(128)]
            .get(mode="promise_in_bounds")
            .reshape(lanes, 64, 128)
        )
        near_up, near_down, routed = tie((near_up, near_down, routed))
        arrived = lax.all_to_all(routed, "tensor", 0, 0, tiled=True)
    with jax.named_scope("gather_grad"):
        across, arrived = tie((across, arrived))
        by_slot = arrived.reshape(lanes, 2, 32, 128)

        def natural(tiles):
            return (
                tiles.reshape(4, 8, 2, 16, 128)
                .transpose(2, 0, 3, 1, 4)
                .reshape(2, piece_rows, size)
            )

        grad_wire = lax.dynamic_index_in_dim(by_slot, 1 - slot, 1, keepdims=False)
        grad_mine = natural(lax.dynamic_index_in_dim(by_slot, slot, 1, keepdims=False))
        grad_wire, grad_mine = tie((grad_wire, grad_mine))
        got_grad = send(grad_wire, partner)
        mine_pieces = around(grad_mine)
        got_grad, mine_pieces = tie((got_grad, mine_pieces))
        got_pieces = around(natural(got_grad))
    with jax.named_scope("early_product"):
        across, _ = tie((across, got_grad))
        early_power, item = statistic_times_basis(info, (same, near_up, across, near_down))
    with jax.named_scope("late_gather"):
        moments = jnp.stack([first_moment, second_moment], axis=1)
        moment_wire = pick(moments, 1 - slot)
        same_late, cross_late, moment_wire, got_pieces = tie(
            (same[1], cross[1], moment_wire, got_pieces)
        )
        other_pieces = (
            cross_late,
            send(same_late, step_up),
            send(cross_late, step_across),
            send(same_late, step_down),
        )
        got_moments = send(moment_wire, partner)
    with jax.named_scope("frame_first"):
        grad, framed_low, gram_rest, tall_rest = frame_first(
            info, mine_pieces + got_pieces, item, early_power
        )
    with jax.named_scope("rotate"):
        other_pieces, got_moments, grad = tie((other_pieces, got_moments, grad))
        moment_rows = jnp.concatenate(
            ordered(slot, pick(moments, slot), got_moments), axis=-2
        )
        returned, keep16, keep32, wire = rotate(
            info, grad, item, other_pieces, moment_rows[0], moment_rows[1]
        )
    with jax.named_scope("exchange"):
        up, down = send(returned, step_up), send(returned, step_down)
        returned_pieces = (returned, up, send(returned, step_across), down)
        got = send(wire, partner)
    with jax.named_scope("frame_second"):
        gram_rest, _ = tie((gram_rest, returned))
        framed_high = frame_second(gram_rest, tall_rest)
        framed = jnp.concatenate([framed_low, framed_high], axis=1)
        left_rows, framed = tie((left_rows, framed))
        back = lax.all_to_all(
            framed.reshape(8, piece_rows, size), "dp", 0, 0, tiled=True
        ).reshape(2, 2, 2, piece_rows, size)
    with jax.named_scope("update"):
        moment_next = jnp.stack(ordered(slot, keep16[0], got[0]))
        second_next = jnp.stack(ordered(slot, keep16[1], got[1]))

        def statistic_next(statistic, kept, came):
            outer = jnp.stack(ordered(slot, kept, came.astype(jnp.float32)))
            return BETA_STATS * statistic + (1.0 - BETA_STATS) * outer

        left_next = statistic_next(left_statistic, keep32[0], got[2])
        right_next = statistic_next(right_statistic, keep32[1], got[3])
        left_rows, left_next = tie((left_rows, left_next))
        mine, theirs = update_rows(info, left_rows, returned_pieces)
        update = jnp.stack(ordered(slot, mine, send(theirs, partner)))
    with jax.named_scope("renew"):
        marker = listed[:, None, None, None]
        renewed = back.transpose(1, 2, 0, 3, 4)
        left_basis_next = jnp.where(marker, renewed[0], left_basis)
        right_basis_next = jnp.where(marker, renewed[1], right_basis)
    return (
        update,
        moment_next,
        second_next,
        left_next,
        right_next,
        left_basis_next,
        right_basis_next,
    )


def solution(mesh):
    held = P("tensor", None, "dp", None)
    in_specs = (P("dp", "tensor", None), P(), P()) + (held,) * 6
    out_specs = (held,) * 7
    return jax.shard_map(body, mesh=mesh, in_specs=in_specs, out_specs=out_specs, check_vma=False)
```
